32 devices in a mesh: groups: 2 (over y), blk: 16 (over z, x, core).
Axes of the slice: x: 2, y: 2, z: 4, core: 2. Of those that a mesh axis runs over, the one named last changes fastest.
Arguments:
- image_embed: bfloat16 [4096, 1152], P(('groups', 'blk')), parts along dimension 0, may hold values from -6 to 6
- report_embed: bfloat16 [4096, 1152], P(('groups', 'blk')), parts along dimension 0, may hold values from -6 to 6
- image_study: int32 [4096], P(('groups', 'blk')), parts along dimension 0, may hold values from 0 to 1023, as said below
- report_study_index: int32 [4096], P(('groups', 'blk')), parts along dimension 0, may hold values from 0 to 1023, as said below
- logit_scale: float32 [2], P('groups'), parts along dimension 0, may hold values from 6 to 16
- logit_bias: float32 [2], P('groups'), parts along dimension 0, may hold values from -6 to -2
Outputs:
- loss: float32 [2], P('groups'), parts along dimension 0
- image_grad: float32 [4096, 1152], P(('groups', 'blk')), parts along dimension 0
- report_grad: float32 [4096, 1152], P(('groups', 'blk')), parts along dimension 0
The draws below stay inside these ranges and needn't reach their ends.
There are 2 independent parts, one for each index of `groups`. The reference program is written for one: setup_inputs(seed, part) draws one part's arguments, and reference() takes and returns one part's arrays. A program takes and returns all parts, laid end to end along the dimension named above; each array names one. Nothing has to cross between parts.
Inputs may be any that keep to these rules, and one draw needn't show every extreme that they name: `image_study`: each study id names exactly two images; image i and report i belong to the same study for most i, and the reports hold the same ids as the images, each exactly twice. `report_study_index`: each study id names exactly two reports.
All inputs are finite; a program needn't handle non-finite values.
Results may differ from the reference program's by a relative error of at most 0.0003.
The reference program's roundings to bfloat16 on the way (of `image_send` and `coeff`) count: a program that leaves them out, or rounds other values in their place, can miss the bound.
Values may be sent and summed in bfloat16 or wider, within the bound.
A program may use at most 128 MiB of HBM per device.

```python
import math
import jax
import jax.numpy as jnp
from jax import lax

D = 1152
B_DEV = 128
PAIRS = 2048


def study_ids(key):
    base = jnp.arange(PAIRS, dtype=jnp.int32) // 2
    return jax.random.permutation(key, base)


def draw_image_study(key, part):
    return study_ids(key)


def draw_report_study_index(key, part):
    shared_study = study_ids(key)
    key = jax.random.fold_in(key, 7)
    flips = (jax.random.randint(key, (PAIRS // 2,), 0, 8) == 0).astype(jnp.int32)
    partner = jnp.arange(PAIRS, dtype=jnp.int32) ^ jnp.repeat(flips, 2)
    return shared_study[partner]


def block_levels(key, extent, split, least, top_value):
    def one(position, blocks):
        heights = jax.random.uniform(jax.random.fold_in(jax.random.fold_in(key, 6), position), (blocks,), jnp.float32, least / len(split), top_value / len(split))
        return jnp.repeat(jnp.exp(heights), extent[position] // blocks).reshape((-1,) + (1,) * (len(extent) - position - 1))

    loudness = one(*split[0])
    for cut in split[1:]:
        loudness = loudness * one(*cut)
    return loudness


def gaussian(stream_key, dims, deviation, reach, split=(), kind=jnp.bfloat16):
    result = jax.random.normal(stream_key, dims, jnp.float32) * deviation
    if len(split) > 0:
        result = block_levels(stream_key, dims, split, -0.22, 0.18) * result
    return jnp.clip(result, min=-reach, max=reach).astype(kind)


def setup_inputs(seed: int = 0, part: int = 0) -> dict:
    keys = jax.random.split(jax.random.key(seed), 7)
    part_keys = jax.random.split(jax.random.fold_in(keys[6], part), 7)
    return {
        "image_embed": gaussian(part_keys[0], (PAIRS, D), 1.0, 6.0, ((0, 16),)),
        "report_embed": gaussian(part_keys[1], (PAIRS, D), 1.0, 6.0, ((0, 16),)),
        "image_study": draw_image_study(jax.random.fold_in(jax.random.fold_in(keys[6], part), 71), part),
        "report_study_index": draw_report_study_index(jax.random.fold_in(jax.random.fold_in(keys[6], part), 71), part),
        "logit_scale": jnp.clip(jnp.exp(jax.random.uniform(part_keys[4], (1,), jnp.float32, math.log(6.0), math.log(16.0))), 6.0, 16.0),
        "logit_bias": jnp.clip(jax.random.uniform(part_keys[5], (1,), jnp.float32, -6.0, -2.0), -6.0, -2.0),
    }


def unit_rows(embed):
    values = embed.astype(jnp.float32)
    norm = jnp.sqrt(lax.optimization_barrier(jnp.sum(values * values, axis=1, keepdims=True)) + 1e-06)
    unit = values / norm
    return (norm, unit, unit.astype(jnp.bfloat16))

def reference(image_embed, report_embed, image_study, report_study_index, logit_scale, logit_bias):
    image_norm, image_unit, image_send = unit_rows(image_embed)
    report_norm, report_unit, report_send = unit_rows(report_embed)
    scale = logit_scale[0]
    bias = logit_bias[0]
    count = PAIRS // B_DEV
    image_blocks = image_send.reshape(count, B_DEV, D)
    study_blocks = image_study.reshape(count, B_DEV)

    def step(carry, input_arrays):
        report_acc, loss_acc = carry
        block_slice, study_labels = input_arrays
        logits = scale * jnp.dot(block_slice, report_send.T, preferred_element_type=jnp.float32) + bias
        pair_sign = jnp.where(study_labels[:, None] == report_study_index[None, :], 1.0, -1.0).astype(jnp.float32)
        loss_acc = loss_acc - jnp.sum(jax.nn.log_sigmoid(pair_sign * logits))
        coeff = (-pair_sign * jax.nn.sigmoid(-pair_sign * logits)).astype(jnp.bfloat16)
        image_part = scale * jnp.dot(coeff, report_send, preferred_element_type=jnp.float32)
        report_acc = report_acc + scale * jnp.dot(coeff.T, block_slice, preferred_element_type=jnp.float32)
        return ((report_acc, loss_acc), image_part)
    start = (jnp.zeros((PAIRS, D), jnp.float32), jnp.zeros((), jnp.float32))
    (report_unit_grad, loss_sum), image_parts = lax.scan(step, start, (image_blocks, study_blocks))
    image_unit_grad = image_parts.reshape(PAIRS, D)
    image_grad = (image_unit_grad - image_unit * lax.optimization_barrier(jnp.sum(image_unit * image_unit_grad, axis=1, keepdims=True))) / image_norm
    report_grad = (report_unit_grad - report_unit * lax.optimization_barrier(jnp.sum(report_unit * report_unit_grad, axis=1, keepdims=True))) / report_norm
    loss = (loss_sum / PAIRS).reshape(1)
    return (loss, image_grad, report_grad)
```

```python
import math

import jax
import jax.numpy as jnp
from jax import lax
from jax.experimental import pallas as pl
from jax.experimental.pallas import tpu as pltpu
from jax.sharding import PartitionSpec as P


def shortened(value):

    def short(part):
        return part.astype(jnp.bfloat16) if part.dtype == jnp.float32 else part

    return jax.tree.map(short, value)


def from_partner(value, axis, stride):
    return lax.ppermute(value, axis, [(i, i ^ 1 << stride) for i in range(lax.axis_size(axis))])


def unit_rows(embed):
    values = embed.astype(jnp.float32)
    norm = jnp.sqrt(jnp.sum(values * values, axis=1, keepdims=True) + 1e-06)
    unit = values / norm
    return (norm, unit, unit.astype(jnp.bfloat16))


def finish(unit_grad, unit, norm):
    return (unit_grad - unit * jnp.sum(unit * unit_grad, axis=1, keepdims=True)) / norm


def placed(upper, mine, theirs):
    return jnp.where(
        upper, jnp.concatenate([theirs, mine], axis=0), jnp.concatenate([mine, theirs], axis=0)
    )


def body(image_embed, report_embed, image_study, report_study_index, logit_scale, logit_bias):
    image_norm, image_unit, image_send = unit_rows(image_embed)
    report_norm, report_unit, report_send = unit_rows(report_embed)
    scale = logit_scale[0]
    bias = logit_bias[0]
    total_bits = lax.axis_size("blk").bit_length() - 1
    image_count = (total_bits + 1) // 2
    report_list = list(range(total_bits - image_count))
    image_list = list(range(total_bits - image_count, total_bits))
    block_position = lax.axis_index("blk")
    images, image_ids = (image_send, image_study)
    for bit in image_list:
        upper = block_position >> bit & 1 == 1
        other_rows, other_ids = (
            from_partner(images, "blk", bit),
            from_partner(shortened(image_ids), "blk", bit).astype(image_ids.dtype),
        )
        images = placed(upper, images, other_rows)
        image_ids = placed(upper, image_ids, other_ids)
    reports, report_index_list = (report_send, report_study_index)
    for bit in report_list:
        upper = block_position >> bit & 1 == 1
        other_rows, other_ids = (
            from_partner(reports, "blk", bit),
            from_partner(shortened(report_index_list), "blk", bit).astype(report_index_list.dtype),
        )
        reports = placed(upper, reports, other_rows)
        report_index_list = placed(upper, report_index_list, other_ids)
    image_total = images.shape[0]
    width = images.shape[1]
    block_rows = math.gcd(image_total, 512)
    block_count = image_total // block_rows
    image_blocks = images.reshape(block_count, block_rows, width)
    id_blocks = image_ids.reshape(block_count, block_rows)

    def step(carry, input_arrays):
        report_acc, loss_acc = carry
        block_slice, study_labels = input_arrays
        logits = (
            scale
            * lax.dot_general(
                block_slice, reports, (((1,), (1,)), ((), ())), preferred_element_type=jnp.float32
            )
            + bias
        )
        pair_sign = jnp.where(
            study_labels[:, None] == report_index_list[None, :], 1.0, -1.0
        ).astype(jnp.float32)
        loss_acc = loss_acc - jnp.sum(jax.nn.log_sigmoid(pair_sign * logits))
        coeff = (-pair_sign * jax.nn.sigmoid(-pair_sign * logits)).astype(jnp.bfloat16)
        image_part = scale * jnp.dot(coeff, reports, preferred_element_type=jnp.float32)
        report_acc = report_acc + scale * lax.dot_general(
            coeff, block_slice, (((0,), (0,)), ((), ())), preferred_element_type=jnp.float32
        )
        return ((report_acc, loss_acc), image_part)

    start = (jnp.zeros((reports.shape[0], width), jnp.float32), jnp.zeros((), jnp.float32))
    (report_part, loss_part), image_parts = lax.scan(step, start, (image_blocks, id_blocks))
    image_part = image_parts.reshape(image_total, width)
    for bit in reversed(image_list):
        upper = block_position >> bit & 1 == 1
        half = image_part.shape[0] // 2
        keep = jnp.where(upper, image_part[half:], image_part[:half])
        give = jnp.where(upper, image_part[:half], image_part[half:])
        image_part = keep + from_partner(give, "blk", bit)
    for bit in reversed(report_list):
        upper = block_position >> bit & 1 == 1
        half = report_part.shape[0] // 2
        keep = jnp.where(upper, report_part[half:], report_part[:half])
        give = jnp.where(upper, report_part[:half], report_part[half:])
        report_part = keep + from_partner(give, "blk", bit)
    total = lax.psum(loss_part, "blk")
    pair_count = image_embed.shape[0] * lax.axis_size("blk")
    loss = (total / pair_count).reshape(1)
    image_grad = finish(image_part, image_unit, image_norm)
    report_grad = finish(report_part, report_unit, report_norm)
    return (loss, image_grad, report_grad)


CORE, ACROSS, NEAR, FAR = (1, 2, 4, 8)
MESH_ID = pl.DeviceIdType.MESH


def tile_kernel(
    image_ref, report_ref, image_id_ref, report_id_ref, scale_ref, bias_ref,
    loss_ref, image_grad_ref, report_grad_ref,
    images, reports, image_ids, report_ids, coeffs, image_part, report_part,
    core_in, far_in, across_in, near_in, far_out, near_out, loss_out, loss_in,
    send_sem, recv_sem,
):
    group = lax.axis_index("groups")
    me = lax.axis_index("blk")
    rows = image_ref.shape[0]

    def partner(bit):
        low = lax.rem(lax.div(me, bit), 2)
        return (group, me + bit - 2 * bit * low)

    def send(number, source, target, bit):
        copy = pltpu.make_async_remote_copy(
            src_ref=source,
            dst_ref=target,
            send_sem=send_sem.at[number],
            recv_sem=recv_sem.at[number],
            device_id=partner(bit),
            device_id_type=MESH_ID,
        )
        copy.start()
        return copy

    barrier = pltpu.get_barrier_semaphore()
    for bit in (CORE, ACROSS, NEAR, FAR):
        pl.semaphore_signal(barrier, inc=1, device_id=partner(bit), device_id_type=MESH_ID)

    def normalised(ref):
        values = ref[...].astype(jnp.float32)
        norm = jnp.sqrt(jnp.sum(values * values, axis=1, keepdims=True) + 1e-06)
        return (norm, values / norm)

    reports[0] = normalised(report_ref)[1].astype(jnp.bfloat16)
    images[0] = normalised(image_ref)[1].astype(jnp.bfloat16)
    image_ids[0] = image_id_ref[...]
    report_ids[0] = report_id_ref[...]
    pl.semaphore_wait(barrier, 4)

    report_near = send(0, reports.at[0], reports.at[2], NEAR)
    report_near_id = send(1, report_ids.at[0], report_ids.at[2], NEAR)
    report_across = send(2, reports.at[0], reports.at[1], ACROSS)
    report_across_id = send(3, report_ids.at[0], report_ids.at[1], ACROSS)
    image_far = send(4, images.at[0], images.at[2], FAR)
    image_far_id = send(5, image_ids.at[0], image_ids.at[2], FAR)
    image_core = send(6, images.at[0], images.at[1], CORE)
    image_core_id = send(7, image_ids.at[0], image_ids.at[1], CORE)

    scale = scale_ref[0]
    bias = bias_ref[0]

    def tile(i, j):
        logits = (
            scale
            * lax.dot_general(
                images[i], reports[j], (((1,), (1,)), ((), ())), preferred_element_type=jnp.float32
            )
            + bias
        )
        across = jnp.broadcast_to(report_ids[j, 0:1, :], (rows, rows))
        down = jnp.broadcast_to(image_ids[i, 0:1, :], (rows, rows)).T
        sign = jnp.where(across == down, 1.0, -1.0).astype(jnp.float32)
        signed = sign * logits
        weight = jnp.exp(-jnp.abs(signed))
        negative = jnp.where(signed >= 0, weight, 1.0) / (1.0 + weight)
        coeffs[i, :, j * rows : (j + 1) * rows] = (-sign * negative).astype(jnp.bfloat16)
        return jnp.maximum(-signed, 0.0) + jnp.log1p(weight)

    image_core.wait()
    image_core_id.wait()
    total = tile(0, 0) + tile(1, 0)
    report_near.wait()
    report_near_id.wait()
    report_diag = send(8, reports.at[2], reports.at[3], ACROSS)
    report_diag_id = send(9, report_ids.at[2], report_ids.at[3], ACROSS)
    total += tile(0, 2) + tile(1, 2)
    report_across.wait()
    report_across_id.wait()
    total += tile(0, 1) + tile(1, 1)
    image_far.wait()
    image_far_id.wait()
    image_diag = send(10, images.at[2], images.at[3], CORE)
    image_diag_id = send(11, image_ids.at[2], image_ids.at[3], CORE)
    total += tile(2, 0) + tile(2, 1) + tile(2, 2)
    image_diag.wait()
    image_diag_id.wait()
    total += tile(3, 0) + tile(3, 1) + tile(3, 2)
    report_diag.wait()
    report_diag_id.wait()
    for i in range(4):
        total += tile(i, 3)

    def image_sum(i):
        out = None
        for j in range(4):
            term = jnp.dot(
                coeffs[i, :, j * rows : (j + 1) * rows], reports[j], preferred_element_type=jnp.float32
            )
            out = term if out is None else out + term
        return scale * out

    def report_sum(j):
        out = None
        for i in range(4):
            term = lax.dot_general(
                coeffs[i, :, j * rows : (j + 1) * rows],
                images[i],
                (((0,), (0,)), ((), ())),
                preferred_element_type=jnp.float32,
            )
            out = term if out is None else out + term
        return scale * out

    report_part[0] = report_sum(3)
    across_first = send(12, report_part.at[0], across_in.at[0], ACROSS)
    image_part[0] = image_sum(3)
    core_first = send(13, image_part.at[0], core_in.at[0], CORE)
    far_sum = image_sum(2)
    core_first.wait_recv()
    far_out[...] = far_sum + core_in[0]
    far_send = send(14, far_out, far_in, FAR)
    report_part[1] = report_sum(1)
    across_second = send(15, report_part.at[1], across_in.at[1], ACROSS)
    image_part[1] = image_sum(1)
    core_second = send(16, image_part.at[1], core_in.at[1], CORE)
    near_sum = report_sum(2)

    loss_out[0] = jnp.sum(total.reshape(rows // 8, 8, rows), axis=0)
    loss_copies = []
    for step, bit in enumerate((CORE, ACROSS, NEAR, FAR)):
        copy = send(18 + step, loss_out.at[step], loss_in.at[step], bit)
        if step == 0:
            own_image = image_sum(0)
        elif step == 1:
            own_report = report_sum(0)
        copy.wait()
        if step < 3:
            loss_out[step + 1] = loss_out[step] + loss_in[step]
        else:
            whole = loss_out[step] + loss_in[step]
    pairs = rows * lax.axis_size("blk")
    loss_ref[...] = jnp.full(loss_ref.shape, jnp.sum(whole) / pairs, jnp.float32)

    across_first.wait_recv()
    near_out[...] = near_sum + across_in[0]
    near_send = send(17, near_out, near_in, NEAR)

    def finish(ref, unit_grad):
        norm, unit = normalised(ref)
        return (unit_grad - unit * jnp.sum(unit * unit_grad, axis=1, keepdims=True)) / norm

    core_second.wait_recv()
    own_image += core_in[1]
    far_send.wait()
    image_grad_ref[...] = finish(image_ref, own_image + far_in[...])
    across_second.wait_recv()
    own_report += across_in[1]
    near_send.wait()
    report_grad_ref[...] = finish(report_ref, own_report + near_in[...])
    across_first.wait_send()
    across_second.wait_send()
    core_first.wait_send()
    core_second.wait_send()


def kernel_body(image_embed, report_embed, image_study, report_study_index, logit_scale, logit_bias):
    rows, width = image_embed.shape
    f32 = jnp.float32

    def id_rows(ids):
        return jnp.broadcast_to(ids[None, :], (8, rows))

    vmem = pl.BlockSpec(memory_space=pltpu.VMEM)
    smem = pl.BlockSpec(memory_space=pltpu.SMEM)
    loss, image_grad, report_grad = pl.pallas_call(
        tile_kernel,
        out_shape=(
            jax.ShapeDtypeStruct((8, 128), f32),
            jax.ShapeDtypeStruct((rows, width), f32),
            jax.ShapeDtypeStruct((rows, width), f32),
        ),
        in_specs=[vmem, vmem, vmem, vmem, smem, smem],
        out_specs=(vmem, vmem, vmem),
        scratch_shapes=[
            pltpu.VMEM((4, rows, width), jnp.bfloat16),
            pltpu.VMEM((4, rows, width), jnp.bfloat16),
            pltpu.VMEM((4, 8, rows), jnp.int32),
            pltpu.VMEM((4, 8, rows), jnp.int32),
            pltpu.VMEM((4, rows, 4 * rows), jnp.bfloat16),
            pltpu.VMEM((2, rows, width), f32),
            pltpu.VMEM((2, rows, width), f32),
            pltpu.VMEM((2, rows, width), f32),
            pltpu.VMEM((rows, width), f32),
            pltpu.VMEM((2, rows, width), f32),
            pltpu.VMEM((rows, width), f32),
            pltpu.VMEM((rows, width), f32),
            pltpu.VMEM((rows, width), f32),
            pltpu.VMEM((4, 8, rows), f32),
            pltpu.VMEM((4, 8, rows), f32),
            pltpu.SemaphoreType.DMA((22,)),
            pltpu.SemaphoreType.DMA((22,)),
        ],
        compiler_params=pltpu.CompilerParams(
            collective_id=0, has_side_effects=True, vmem_limit_bytes=48 * 1024 * 1024
        ),
    )(
        image_embed,
        report_embed,
        id_rows(image_study),
        id_rows(report_study_index),
        logit_scale,
        logit_bias,
    )
    return (loss[0, :1], image_grad, report_grad)


def solution(mesh):
    return jax.shard_map(
        kernel_body if mesh.shape["blk"] == 16 else body,
        mesh=mesh,
        in_specs=(
            P(("groups", "blk"), None),
            P(("groups", "blk"), None),
            P(("groups", "blk")),
            P(("groups", "blk")),
            P("groups"),
            P("groups"),
        ),
        out_specs=(P("groups"), P(("groups", "blk"), None), P(("groups", "blk"), None)),
        check_vma=False,
    )
```

```python
import math

import jax
import jax.numpy as jnp
from jax import lax
from jax.experimental import pallas as pl
from jax.experimental.pallas import tpu as pltpu
from jax.sharding import PartitionSpec as P


def shortened(value):

    def short(part):
        return part.astype(jnp.bfloat16) if part.dtype == jnp.float32 else part

    return jax.tree.map(short, value)


def from_partner(value, axis, stride):
    return lax.ppermute(value, axis, [(i, i ^ 1 << stride) for i in range(lax.axis_size(axis))])


def unit_rows(embed):
    values = embed.astype(jnp.float32)
    norm = jnp.sqrt(jnp.sum(values * values, axis=1, keepdims=True) + 1e-06)
    unit = values / norm
    return (norm, unit, unit.astype(jnp.bfloat16))


def finish(unit_grad, unit, norm):
    return (unit_grad - unit * jnp.sum(unit * unit_grad, axis=1, keepdims=True)) / norm


def placed(upper, mine, theirs):
    return jnp.where(
        upper, jnp.concatenate([theirs, mine], axis=0), jnp.concatenate([mine, theirs], axis=0)
    )


def body(image_embed, report_embed, image_study, report_study_index, logit_scale, logit_bias):
    image_norm, image_unit, image_send = unit_rows(image_embed)
    report_norm, report_unit, report_send = unit_rows(report_embed)
    scale = logit_scale[0]
    bias = logit_bias[0]
    total_bits = lax.axis_size("blk").bit_length() - 1
    image_count = (total_bits + 1) // 2
    report_list = list(range(total_bits - image_count))
    image_list = list(range(total_bits - image_count, total_bits))
    block_position = lax.axis_index("blk")
    images, image_ids = (image_send, image_study)
    for bit in image_list:
        upper = block_position >> bit & 1 == 1
        other_rows, other_ids = (
            from_partner(images, "blk", bit),
            from_partner(shortened(image_ids), "blk", bit).astype(image_ids.dtype),
        )
        images = placed(upper, images, other_rows)
        image_ids = placed(upper, image_ids, other_ids)
    reports, report_index_list = (report_send, report_study_index)
    for bit in report_list:
        upper = block_position >> bit & 1 == 1
        other_rows, other_ids = (
            from_partner(reports, "blk", bit),
            from_partner(shortened(report_index_list), "blk", bit).astype(report_index_list.dtype),
        )
        reports = placed(upper, reports, other_rows)
        report_index_list = placed(upper, report_index_list, other_ids)
    image_total = images.shape[0]
    width = images.shape[1]
    block_rows = math.gcd(image_total, 512)
    block_count = image_total // block_rows
    image_blocks = images.reshape(block_count, block_rows, width)
    id_blocks = image_ids.reshape(block_count, block_rows)

    def step(carry, input_arrays):
        report_acc, loss_acc = carry
        block_slice, study_labels = input_arrays
        logits = (
            scale
            * lax.dot_general(
                block_slice, reports, (((1,), (1,)), ((), ())), preferred_element_type=jnp.float32
            )
            + bias
        )
        pair_sign = jnp.where(
            study_labels[:, None] == report_index_list[None, :], 1.0, -1.0
        ).astype(jnp.float32)
        loss_acc = loss_acc - jnp.sum(jax.nn.log_sigmoid(pair_sign * logits))
        coeff = (-pair_sign * jax.nn.sigmoid(-pair_sign * logits)).astype(jnp.bfloat16)
        image_part = scale * jnp.dot(coeff, reports, preferred_element_type=jnp.float32)
        report_acc = report_acc + scale * lax.dot_general(
            coeff, block_slice, (((0,), (0,)), ((), ())), preferred_element_type=jnp.float32
        )
        return ((report_acc, loss_acc), image_part)

    start = (jnp.zeros((reports.shape[0], width), jnp.float32), jnp.zeros((), jnp.float32))
    (report_part, loss_part), image_parts = lax.scan(step, start, (image_blocks, id_blocks))
    image_part = image_parts.reshape(image_total, width)
    for bit in reversed(image_list):
        upper = block_position >> bit & 1 == 1
        half = image_part.shape[0] // 2
        keep = jnp.where(upper, image_part[half:], image_part[:half])
        give = jnp.where(upper, image_part[:half], image_part[half:])
        image_part = keep + from_partner(give, "blk", bit)
    for bit in reversed(report_list):
        upper = block_position >> bit & 1 == 1
        half = report_part.shape[0] // 2
        keep = jnp.where(upper, report_part[half:], report_part[:half])
        give = jnp.where(upper, report_part[:half], report_part[half:])
        report_part = keep + from_partner(give, "blk", bit)
    total = lax.psum(loss_part, "blk")
    pair_count = image_embed.shape[0] * lax.axis_size("blk")
    loss = (total / pair_count).reshape(1)
    image_grad = finish(image_part, image_unit, image_norm)
    report_grad = finish(report_part, report_unit, report_norm)
    return (loss, image_grad, report_grad)


CORE, ACROSS, NEAR, FAR = (1, 2, 4, 8)
PIECES = 4
TOP = 32767.0
MESH_ID = pl.DeviceIdType.MESH


def encode(value, code_ref, step_ref):
    peak = jnp.maximum(jnp.max(jnp.abs(value), axis=1, keepdims=True), 1e-30)
    code_ref[...] = jnp.round(value * (TOP / peak)).astype(jnp.int32).astype(jnp.int16)
    rows = value.shape[0]
    step_ref[...] = jnp.broadcast_to(peak * (1.0 / TOP), (rows, rows)).T[:8]


def decode(code_ref, step_ref):
    code = code_ref[...].astype(jnp.int32).astype(jnp.float32)
    rows = code.shape[0]
    return code * jnp.broadcast_to(step_ref[0:1, :], (rows, rows)).T[:, :1]


def tile_kernel(
    image_hbm, report_hbm, image_id_ref, report_id_ref, scale_ref, bias_ref,
    loss_ref, image_grad_ref, report_grad_ref,
    image_ref, report_ref,
    images, reports, image_ids, report_ids, coeffs, image_part, core_in,
    codes_out, codes_in, steps_out, steps_in, loss_out, loss_in,
    load_sem, send_sem, recv_sem,
):
    group = lax.axis_index("groups")
    me = lax.axis_index("blk")
    rows = image_ref.shape[0]
    piece = rows // PIECES

    def partner(bit):
        low = lax.rem(lax.div(me, bit), 2)
        return (group, me + bit - 2 * bit * low)

    def send(number, source, target, bit):
        copy = pltpu.make_async_remote_copy(
            src_ref=source,
            dst_ref=target,
            send_sem=send_sem.at[number],
            recv_sem=recv_sem.at[number],
            device_id=partner(bit),
            device_id_type=MESH_ID,
        )
        copy.start()
        return copy

    report_load = pltpu.make_async_copy(report_hbm, report_ref, load_sem.at[0])
    report_load.start()
    image_load = pltpu.make_async_copy(image_hbm, image_ref, load_sem.at[1])
    image_load.start()
    barrier = pltpu.get_barrier_semaphore()
    for bit in (CORE, ACROSS, NEAR, FAR):
        pl.semaphore_signal(barrier, inc=1, device_id=partner(bit), device_id_type=MESH_ID)

    def normalised(ref):
        values = ref[...].astype(jnp.float32)
        norm = jnp.sqrt(jnp.sum(values * values, axis=1, keepdims=True) + 1e-06)
        return (norm, values / norm)

    report_load.wait()
    reports[0] = normalised(report_ref)[1].astype(jnp.bfloat16)
    image_load.wait()
    images[0] = normalised(image_ref)[1].astype(jnp.bfloat16)
    image_ids[0] = jnp.broadcast_to(image_id_ref[...], (8, rows))
    report_ids[0] = jnp.broadcast_to(report_id_ref[...], (8, rows))
    pl.semaphore_wait(barrier, 4)

    def part(k):
        return pl.ds(k * piece, piece)

    report_near = [
        send(32 + k, reports.at[0, part(k)], reports.at[2, part(k)], NEAR) for k in range(PIECES)
    ]
    report_near_id = send(1, report_ids.at[0], report_ids.at[2], NEAR)
    report_across = send(2, reports.at[0], reports.at[1], ACROSS)
    report_across_id = send(3, report_ids.at[0], report_ids.at[1], ACROSS)
    image_far = send(4, images.at[0], images.at[2], FAR)
    image_far_id = send(5, image_ids.at[0], image_ids.at[2], FAR)
    image_core = send(6, images.at[0], images.at[1], CORE)
    image_core_id = send(7, image_ids.at[0], image_ids.at[1], CORE)

    scale = scale_ref[0]
    bias = bias_ref[0]

    def tile(i, j):
        logits = (
            scale
            * lax.dot_general(
                images[i], reports[j], (((1,), (1,)), ((), ())), preferred_element_type=jnp.float32
            )
            + bias
        )
        across = jnp.broadcast_to(report_ids[j, 0:1, :], (rows, rows))
        down = jnp.broadcast_to(image_ids[i, 0:1, :], (rows, rows)).T
        sign = jnp.where(across == down, 1.0, -1.0).astype(jnp.float32)
        signed = sign * logits
        weight = jnp.exp(-jnp.abs(signed))
        negative = jnp.where(signed >= 0, weight, 1.0) / (1.0 + weight)
        coeffs[i, :, j * rows : (j + 1) * rows] = (-sign * negative).astype(jnp.bfloat16)
        return jnp.maximum(-signed, 0.0) + jnp.log1p(weight)

    image_core.wait()
    image_core_id.wait()
    total = tile(0, 0) + tile(1, 0)
    report_near_id.wait()
    report_diag_id = send(9, report_ids.at[2], report_ids.at[3], ACROSS)
    report_diag = []
    for k in range(PIECES):
        report_near[k].wait()
        report_diag.append(
            send(32 + PIECES + k, reports.at[2, part(k)], reports.at[3, part(k)], ACROSS)
        )
    total += tile(0, 2) + tile(1, 2)
    report_across.wait()
    report_across_id.wait()
    total += tile(0, 1) + tile(1, 1)
    image_far.wait()
    image_far_id.wait()
    image_diag = send(10, images.at[2], images.at[3], CORE)
    image_diag_id = send(11, image_ids.at[2], image_ids.at[3], CORE)
    total += tile(2, 0) + tile(2, 1) + tile(2, 2)
    image_diag.wait()
    image_diag_id.wait()
    total += tile(3, 0) + tile(3, 1) + tile(3, 2)
    for copy in report_diag:
        copy.wait()
    report_diag_id.wait()
    for i in range(4):
        total += tile(i, 3)

    def image_sum(i):
        out = None
        for j in range(4):
            term = jnp.dot(
                coeffs[i, :, j * rows : (j + 1) * rows], reports[j], preferred_element_type=jnp.float32
            )
            out = term if out is None else out + term
        return scale * out

    def report_sum(j):
        out = None
        for i in range(4):
            term = lax.dot_general(
                coeffs[i, :, j * rows : (j + 1) * rows],
                images[i],
                (((0,), (0,)), ((), ())),
                preferred_element_type=jnp.float32,
            )
            out = term if out is None else out + term
        return scale * out

    def send_coded(number, value, bit):
        encode(value, codes_out.at[number], steps_out.at[number])
        return (
            send(12 + 2 * number, steps_out.at[number], steps_in.at[number], bit),
            send(13 + 2 * number, codes_out.at[number], codes_in.at[number], bit),
        )

    def receive(copies, number):
        for copy in copies:
            copy.wait()
        return decode(codes_in.at[number], steps_in.at[number])

    across_first = send_coded(0, report_sum(3), ACROSS)
    image_part[0] = image_sum(3)
    core_first = send(20, image_part.at[0], core_in.at[0], CORE)
    far_sum = image_sum(2)
    core_first.wait()
    far = send_coded(1, far_sum + core_in[0], FAR)
    across_sum = report_sum(1)
    near_sum = report_sum(2)
    near = send_coded(2, near_sum + receive(across_first, 0), NEAR)
    across_second = send_coded(3, across_sum, ACROSS)
    image_part[1] = image_sum(1)
    core_second = send(21, image_part.at[1], core_in.at[1], CORE)

    loss_out[0] = jnp.sum(total.reshape(rows // 8, 8, rows), axis=0)
    loss_copies = []
    for step, bit in enumerate((CORE, ACROSS, NEAR, FAR)):
        copy = send(22 + step, loss_out.at[step], loss_in.at[step], bit)
        if step == 0:
            own_image = image_sum(0)
        elif step == 1:
            own_report = report_sum(0)
        copy.wait()
        if step < 3:
            loss_out[step + 1] = loss_out[step] + loss_in[step]
        else:
            whole = loss_out[step] + loss_in[step]
    pairs = rows * lax.axis_size("blk")
    loss_ref[...] = jnp.full(loss_ref.shape, jnp.sum(whole) / pairs, jnp.float32)

    def finish(ref, unit_grad):
        norm, unit = normalised(ref)
        return (unit_grad - unit * jnp.sum(unit * unit_grad, axis=1, keepdims=True)) / norm

    core_second.wait()
    own_image += core_in[1]
    image_grad_ref[...] = finish(image_ref, own_image + receive(far, 1))
    own_report += receive(across_second, 3)
    report_grad_ref[...] = finish(report_ref, own_report + receive(near, 2))


def kernel_body(image_embed, report_embed, image_study, report_study_index, logit_scale, logit_bias):
    rows, width = image_embed.shape
    f32 = jnp.float32

    vmem = pl.BlockSpec(memory_space=pltpu.VMEM)
    hbm = pl.BlockSpec(memory_space=pl.ANY)
    smem = pl.BlockSpec(memory_space=pltpu.SMEM)
    loss, image_grad, report_grad = pl.pallas_call(
        tile_kernel,
        out_shape=(
            jax.ShapeDtypeStruct((8, 128), f32),
            jax.ShapeDtypeStruct((rows, width), f32),
            jax.ShapeDtypeStruct((rows, width), f32),
        ),
        in_specs=[hbm, hbm, vmem, vmem, smem, smem],
        out_specs=(vmem, vmem, vmem),
        scratch_shapes=[
            pltpu.VMEM((rows, width), jnp.bfloat16),
            pltpu.VMEM((rows, width), jnp.bfloat16),
            pltpu.VMEM((4, rows, width), jnp.bfloat16),
            pltpu.VMEM((4, rows, width), jnp.bfloat16),
            pltpu.VMEM((4, 8, rows), jnp.int32),
            pltpu.VMEM((4, 8, rows), jnp.int32),
            pltpu.VMEM((4, rows, 4 * rows), jnp.bfloat16),
            pltpu.VMEM((2, rows, width), f32),
            pltpu.VMEM((2, rows, width), f32),
            pltpu.VMEM((4, rows, width), jnp.int16),
            pltpu.VMEM((4, rows, width), jnp.int16),
            pltpu.VMEM((4, 8, rows), f32),
            pltpu.VMEM((4, 8, rows), f32),
            pltpu.VMEM((4, 8, rows), f32),
            pltpu.VMEM((4, 8, rows), f32),
            pltpu.SemaphoreType.DMA((2,)),
            pltpu.SemaphoreType.DMA((32 + 2 * PIECES,)),
            pltpu.SemaphoreType.DMA((32 + 2 * PIECES,)),
        ],
        compiler_params=pltpu.CompilerParams(
            collective_id=0, has_side_effects=True, vmem_limit_bytes=48 * 1024 * 1024
        ),
    )(
        image_embed,
        report_embed,
        image_study.reshape(1, rows),
        report_study_index.reshape(1, rows),
        logit_scale,
        logit_bias,
    )
    return (loss[0, :1], image_grad, report_grad)


def solution(mesh):
    return jax.shard_map(
        kernel_body if mesh.shape["blk"] == 16 else body,
        mesh=mesh,
        in_specs=(
            P(("groups", "blk"), None),
            P(("groups", "blk"), None),
            P(("groups", "blk")),
            P(("groups", "blk")),
            P("groups"),
            P("groups"),
        ),
        out_specs=(P("groups"), P(("groups", "blk"), None), P(("groups", "blk"), None)),
        check_vma=False,
    )
```

```python
import math

import jax
import jax.numpy as jnp
from jax import lax
from jax.experimental import pallas as pl
from jax.experimental.pallas import tpu as pltpu
from jax.sharding import PartitionSpec as P


def shortened(value):

    def short(part):
        return part.astype(jnp.bfloat16) if part.dtype == jnp.float32 else part

    return jax.tree.map(short, value)


def from_partner(value, axis, stride):
    return lax.ppermute(value, axis, [(i, i ^ 1 << stride) for i in range(lax.axis_size(axis))])


def unit_rows(embed):
    values = embed.astype(jnp.float32)
    norm = jnp.sqrt(jnp.sum(values * values, axis=1, keepdims=True) + 1e-06)
    unit = values / norm
    return (norm, unit, unit.astype(jnp.bfloat16))


def finish(unit_grad, unit, norm):
    return (unit_grad - unit * jnp.sum(unit * unit_grad, axis=1, keepdims=True)) / norm


def placed(upper, mine, theirs):
    return jnp.where(
        upper, jnp.concatenate([theirs, mine], axis=0), jnp.concatenate([mine, theirs], axis=0)
    )


def body(image_embed, report_embed, image_study, report_study_index, logit_scale, logit_bias):
    image_norm, image_unit, image_send = unit_rows(image_embed)
    report_norm, report_unit, report_send = unit_rows(report_embed)
    scale = logit_scale[0]
    bias = logit_bias[0]
    total_bits = lax.axis_size("blk").bit_length() - 1
    image_count = (total_bits + 1) // 2
    report_list = list(range(total_bits - image_count))
    image_list = list(range(total_bits - image_count, total_bits))
    block_position = lax.axis_index("blk")
    images, image_ids = (image_send, image_study)
    for bit in image_list:
        upper = block_position >> bit & 1 == 1
        other_rows, other_ids = (
            from_partner(images, "blk", bit),
            from_partner(shortened(image_ids), "blk", bit).astype(image_ids.dtype),
        )
        images = placed(upper, images, other_rows)
        image_ids = placed(upper, image_ids, other_ids)
    reports, report_index_list = (report_send, report_study_index)
    for bit in report_list:
        upper = block_position >> bit & 1 == 1
        other_rows, other_ids = (
            from_partner(reports, "blk", bit),
            from_partner(shortened(report_index_list), "blk", bit).astype(report_index_list.dtype),
        )
        reports = placed(upper, reports, other_rows)
        report_index_list = placed(upper, report_index_list, other_ids)
    image_total = images.shape[0]
    width = images.shape[1]
    block_rows = math.gcd(image_total, 512)
    block_count = image_total // block_rows
    image_blocks = images.reshape(block_count, block_rows, width)
    id_blocks = image_ids.reshape(block_count, block_rows)

    def step(carry, input_arrays):
        report_acc, loss_acc = carry
        block_slice, study_labels = input_arrays
        logits = (
            scale
            * lax.dot_general(
                block_slice, reports, (((1,), (1,)), ((), ())), preferred_element_type=jnp.float32
            )
            + bias
        )
        pair_sign = jnp.where(
            study_labels[:, None] == report_index_list[None, :], 1.0, -1.0
        ).astype(jnp.float32)
        loss_acc = loss_acc - jnp.sum(jax.nn.log_sigmoid(pair_sign * logits))
        coeff = (-pair_sign * jax.nn.sigmoid(-pair_sign * logits)).astype(jnp.bfloat16)
        image_part = scale * jnp.dot(coeff, reports, preferred_element_type=jnp.float32)
        report_acc = report_acc + scale * lax.dot_general(
            coeff, block_slice, (((0,), (0,)), ((), ())), preferred_element_type=jnp.float32
        )
        return ((report_acc, loss_acc), image_part)

    start = (jnp.zeros((reports.shape[0], width), jnp.float32), jnp.zeros((), jnp.float32))
    (report_part, loss_part), image_parts = lax.scan(step, start, (image_blocks, id_blocks))
    image_part = image_parts.reshape(image_total, width)
    for bit in reversed(image_list):
        upper = block_position >> bit & 1 == 1
        half = image_part.shape[0] // 2
        keep = jnp.where(upper, image_part[half:], image_part[:half])
        give = jnp.where(upper, image_part[:half], image_part[half:])
        image_part = keep + from_partner(give, "blk", bit)
    for bit in reversed(report_list):
        upper = block_position >> bit & 1 == 1
        half = report_part.shape[0] // 2
        keep = jnp.where(upper, report_part[half:], report_part[:half])
        give = jnp.where(upper, report_part[:half], report_part[half:])
        report_part = keep + from_partner(give, "blk", bit)
    total = lax.psum(loss_part, "blk")
    pair_count = image_embed.shape[0] * lax.axis_size("blk")
    loss = (total / pair_count).reshape(1)
    image_grad = finish(image_part, image_unit, image_norm)
    report_grad = finish(report_part, report_unit, report_norm)
    return (loss, image_grad, report_grad)


CORE, ACROSS, NEAR, FAR = (1, 2, 4, 8)
PIECES = 4
TOP = 32767.0
MESH_ID = pl.DeviceIdType.MESH


def turned(column, rows):
    square = jnp.broadcast_to(column, (column.shape[0], rows))
    return jnp.concatenate([square] * (rows // column.shape[0]), axis=0).T


def encode(value, code_ref, step_ref):
    peak = jnp.maximum(jnp.max(jnp.abs(value), axis=1, keepdims=True), 1e-30)
    code_ref[...] = jnp.round(value * (TOP / peak)).astype(jnp.int32).astype(jnp.int16)
    step_ref[...] = turned(peak * (1.0 / TOP), step_ref.shape[1])[:8]


def decode(code_ref, step_ref):
    code = code_ref[...].astype(jnp.int32).astype(jnp.float32)
    rows = step_ref.shape[1]
    step = jnp.broadcast_to(step_ref[0:1, :], (rows, rows)).T[: code.shape[0], :1]
    return code * step


def tile_kernel(
    image_hbm, report_hbm, image_id_hbm, report_id_hbm, scale_ref, bias_ref,
    loss_ref, image_grad_ref, report_grad_ref,
    image_ref, report_ref, image_id_ref, report_id_ref,
    images, reports, image_ids, report_ids, coeffs, image_part, report_part, core_in,
    codes_out, codes_in, steps_out, steps_in, loss_out, loss_in,
    load_sem, send_sem, recv_sem,
):
    group = lax.axis_index("groups")
    me = lax.axis_index("blk")
    rows = image_ref.shape[0]
    piece = rows // PIECES

    def partner(bit):
        low = lax.rem(lax.div(me, bit), 2)
        return (group, me + bit - 2 * bit * low)

    def send(number, source, target, bit):
        copy = pltpu.make_async_remote_copy(
            src_ref=source,
            dst_ref=target,
            send_sem=send_sem.at[number],
            recv_sem=recv_sem.at[number],
            device_id=partner(bit),
            device_id_type=MESH_ID,
        )
        copy.start()
        return copy

    loads = []
    for source, target in (
        (report_hbm, report_ref),
        (image_hbm, image_ref),
        (report_id_hbm, report_id_ref),
        (image_id_hbm, image_id_ref),
    ):
        loads.append(pltpu.make_async_copy(source, target, load_sem.at[len(loads)]))
        loads[-1].start()
    barrier = pltpu.get_barrier_semaphore()
    for bit in (CORE, ACROSS, NEAR, FAR):
        pl.semaphore_signal(barrier, inc=1, device_id=partner(bit), device_id_type=MESH_ID)

    def normalised(ref):
        values = ref[...].astype(jnp.float32)
        norm = jnp.sqrt(jnp.sum(values * values, axis=1, keepdims=True) + 1e-06)
        return (norm, values / norm)

    loads[0].wait()
    reports[0] = normalised(report_ref)[1].astype(jnp.bfloat16)
    loads[1].wait()
    images[0] = normalised(image_ref)[1].astype(jnp.bfloat16)
    loads[2].wait()
    loads[3].wait()
    image_ids[0] = jnp.broadcast_to(image_id_ref[...], (8, rows))
    report_ids[0] = jnp.broadcast_to(report_id_ref[...], (8, rows))
    pl.semaphore_wait(barrier, 4)

    def part(k):
        return pl.ds(k * piece, piece)

    def near_piece(k):
        return send(32 + k, reports.at[0, part(k)], reports.at[2, part(k)], NEAR)

    report_near = [near_piece(0), near_piece(1)]
    report_near_id = send(1, report_ids.at[0], report_ids.at[2], NEAR)
    report_across = send(2, reports.at[0], reports.at[1], ACROSS)
    report_across_id = send(3, report_ids.at[0], report_ids.at[1], ACROSS)
    image_far = send(4, images.at[0], images.at[2], FAR)
    image_far_id = send(5, image_ids.at[0], image_ids.at[2], FAR)
    image_core = send(6, images.at[0], images.at[1], CORE)
    image_core_id = send(7, image_ids.at[0], image_ids.at[1], CORE)

    scale = scale_ref[0]
    bias = bias_ref[0]

    def tile(i, j):
        logits = (
            scale
            * lax.dot_general(
                images[i], reports[j], (((1,), (1,)), ((), ())), preferred_element_type=jnp.float32
            )
            + bias
        )
        across = jnp.broadcast_to(report_ids[j, 0:1, :], (rows, rows))
        down = jnp.broadcast_to(image_ids[i, 0:1, :], (rows, rows)).T
        sign = jnp.where(across == down, 1.0, -1.0).astype(jnp.float32)
        signed = sign * logits
        weight = jnp.exp(-jnp.abs(signed))
        negative = jnp.where(signed >= 0, weight, 1.0) / (1.0 + weight)
        coeffs[i, :, j * rows : (j + 1) * rows] = (-sign * negative).astype(jnp.bfloat16)
        return jnp.maximum(-signed, 0.0) + jnp.log1p(weight)

    image_core.wait()
    image_core_id.wait()
    total = tile(0, 0) + tile(1, 0)
    report_near_id.wait()
    report_diag_id = send(9, report_ids.at[2], report_ids.at[3], ACROSS)
    report_diag = []
    for k in range(PIECES):
        report_near[k].wait()
        if k + 2 < PIECES:
            report_near.append(near_piece(k + 2))
        report_diag.append(
            send(32 + PIECES + k, reports.at[2, part(k)], reports.at[3, part(k)], ACROSS)
        )
    total += tile(0, 2) + tile(1, 2)
    report_across.wait()
    report_across_id.wait()
    total += tile(0, 1) + tile(1, 1)
    image_far.wait()
    image_far_id.wait()
    image_diag = send(10, images.at[2], images.at[3], CORE)
    image_diag_id = send(11, image_ids.at[2], image_ids.at[3], CORE)
    total += tile(2, 0) + tile(2, 1) + tile(2, 2)
    image_diag.wait()
    image_diag_id.wait()
    total += tile(3, 0) + tile(3, 1) + tile(3, 2)
    def report_sum(j):
        out = None
        for i in range(4):
            term = lax.dot_general(
                coeffs[i, :, j * rows : (j + 1) * rows],
                images[i],
                (((0,), (0,)), ((), ())),
                preferred_element_type=jnp.float32,
            )
            out = term if out is None else out + term
        return scale * out

    report_part[0] = report_sum(1)
    report_part[1] = report_sum(2)
    early = reports[:3].reshape(3 * rows, images.shape[2])
    for i in (3, 2, 1, 0):
        image_part[i] = scale * jnp.dot(
            coeffs[i, :, : 3 * rows], early, preferred_element_type=jnp.float32
        )

    def image_sum(i):
        return image_part[i] + scale * jnp.dot(
            coeffs[i, :, 3 * rows :], reports[3], preferred_element_type=jnp.float32
        )

    for copy in report_diag:
        copy.wait()
    report_diag_id.wait()
    for i in range(4):
        total += tile(i, 3)

    def send_coded(number, value, bit):
        slot, first = divmod(number, PIECES)
        height = value.shape[0]
        lines = pl.ds(first * height, height)
        encode(value, codes_out.at[slot, lines], steps_out.at[number])
        return [
            send(40 + 2 * number, steps_out.at[number], steps_in.at[number], bit),
            send(
                41 + 2 * number, codes_out.at[slot, lines], codes_in.at[slot, lines], bit
            ),
        ]

    def receive(copies, number, height):
        slot, first = divmod(number, PIECES)
        for copy in copies:
            copy.wait()
        return decode(codes_in.at[slot, pl.ds(first * height, height)], steps_in.at[number])

    reports_sum = report_sum(3)
    pieces = [reports_sum[k * piece : (k + 1) * piece] for k in range(PIECES)]
    across_first = [send_coded(k, pieces[k], ACROSS) for k in range(2)]
    image_part[3] = image_sum(3)
    core_first = send(20, image_part.at[3], core_in.at[0], CORE)
    for k in range(2, PIECES):
        report_part[2, part(k)] = pieces[k]
    image_part[2] = image_sum(2)
    core_first.wait()
    far = send_coded(3 * PIECES, image_part[2] + core_in[0], FAR)
    near = []
    for k in range(PIECES):
        landed = receive(across_first[k], k, piece)
        near.append(send_coded(PIECES + k, report_part[1, part(k)] + landed, NEAR))
        if k + 2 < PIECES:
            across_first.append(send_coded(k + 2, report_part[2, part(k + 2)], ACROSS))
    across_second = send_coded(2 * PIECES, report_part[0], ACROSS)
    image_part[1] = image_sum(1)
    core_second = send(21, image_part.at[1], core_in.at[1], CORE)

    loss_out[0] = jnp.sum(total.reshape(rows // 8, 8, rows), axis=0)
    loss_copies = []
    for step, bit in enumerate((CORE, ACROSS, NEAR, FAR)):
        copy = send(22 + step, loss_out.at[step], loss_in.at[step], bit)
        if step == 0:
            own_image = image_sum(0)
        elif step == 1:
            own_report = report_sum(0)
        copy.wait()
        if step < 3:
            loss_out[step + 1] = loss_out[step] + loss_in[step]
        else:
            whole = loss_out[step] + loss_in[step]
    pairs = rows * lax.axis_size("blk")
    loss_ref[...] = jnp.full(loss_ref.shape, jnp.sum(whole) / pairs, jnp.float32)

    def finish(ref, unit_grad):
        norm, unit = normalised(ref)
        return (unit_grad - unit * jnp.sum(unit * unit_grad, axis=1, keepdims=True)) / norm

    core_second.wait()
    own_image += core_in[1]
    image_grad_ref[...] = finish(image_ref, own_image + receive(far, 3 * PIECES, rows))
    own_report += receive(across_second, 2 * PIECES, rows)
    for k in range(PIECES):
        report_part[0, part(k)] = receive(near[k], PIECES + k, piece)
    report_grad_ref[...] = finish(report_ref, own_report + report_part[0])


def kernel_body(image_embed, report_embed, image_study, report_study_index, logit_scale, logit_bias):
    rows, width = image_embed.shape
    f32 = jnp.float32

    vmem = pl.BlockSpec(memory_space=pltpu.VMEM)
    hbm = pl.BlockSpec(memory_space=pl.ANY)
    smem = pl.BlockSpec(memory_space=pltpu.SMEM)
    loss, image_grad, report_grad = pl.pallas_call(
        tile_kernel,
        out_shape=(
            jax.ShapeDtypeStruct((8, 128), f32),
            jax.ShapeDtypeStruct((rows, width), f32),
            jax.ShapeDtypeStruct((rows, width), f32),
        ),
        in_specs=[hbm, hbm, hbm, hbm, smem, smem],
        out_specs=(vmem, vmem, vmem),
        scratch_shapes=[
            pltpu.VMEM((rows, width), jnp.bfloat16),
            pltpu.VMEM((rows, width), jnp.bfloat16),
            pltpu.VMEM((1, rows), jnp.int32),
            pltpu.VMEM((1, rows), jnp.int32),
            pltpu.VMEM((4, rows, width), jnp.bfloat16),
            pltpu.VMEM((4, rows, width), jnp.bfloat16),
            pltpu.VMEM((4, 8, rows), jnp.int32),
            pltpu.VMEM((4, 8, rows), jnp.int32),
            pltpu.VMEM((4, rows, 4 * rows), jnp.bfloat16),
            pltpu.VMEM((4, rows, width), f32),
            pltpu.VMEM((3, rows, width), f32),
            pltpu.VMEM((2, rows, width), f32),
            pltpu.VMEM((4, rows, width), jnp.int16),
            pltpu.VMEM((4, rows, width), jnp.int16),
            pltpu.VMEM((4 * PIECES, 8, rows), f32),
            pltpu.VMEM((4 * PIECES, 8, rows), f32),
            pltpu.VMEM((4, 8, rows), f32),
            pltpu.VMEM((4, 8, rows), f32),
            pltpu.SemaphoreType.DMA((4,)),
            pltpu.SemaphoreType.DMA((40 + 8 * PIECES,)),
            pltpu.SemaphoreType.DMA((40 + 8 * PIECES,)),
        ],
        compiler_params=pltpu.CompilerParams(
            collective_id=0, has_side_effects=True, vmem_limit_bytes=60 * 1024 * 1024
        ),
    )(
        image_embed,
        report_embed,
        image_study.reshape(1, rows),
        report_study_index.reshape(1, rows),
        logit_scale,
        logit_bias,
    )
    return (loss[0, :1], image_grad, report_grad)


def solution(mesh):
    return jax.shard_map(
        kernel_body if mesh.shape["blk"] == 16 else body,
        mesh=mesh,
        in_specs=(
            P(("groups", "blk"), None),
            P(("groups", "blk"), None),
            P(("groups", "blk")),
            P(("groups", "blk")),
            P("groups"),
            P("groups"),
        ),
        out_specs=(P("groups"), P(("groups", "blk"), None), P(("groups", "blk"), None)),
        check_vma=False,
    )
```

```python
import math

import jax
import jax.numpy as jnp
from jax import lax
from jax.experimental import pallas as pl
from jax.experimental.pallas import tpu as pltpu
from jax.sharding import PartitionSpec as P


def shortened(value):

    def short(part):
        return part.astype(jnp.bfloat16) if part.dtype == jnp.float32 else part

    return jax.tree.map(short, value)


def from_partner(value, axis, stride):
    return lax.ppermute(value, axis, [(i, i ^ 1 << stride) for i in range(lax.axis_size(axis))])


def unit_rows(embed):
    values = embed.astype(jnp.float32)
    norm = jnp.sqrt(jnp.sum(values * values, axis=1, keepdims=True) + 1e-06)
    unit = values / norm
    return (norm, unit, unit.astype(jnp.bfloat16))


def finish(unit_grad, unit, norm):
    return (unit_grad - unit * jnp.sum(unit * unit_grad, axis=1, keepdims=True)) / norm


def placed(upper, mine, theirs):
    return jnp.where(
        upper, jnp.concatenate([theirs, mine], axis=0), jnp.concatenate([mine, theirs], axis=0)
    )


def body(image_embed, report_embed, image_study, report_study_index, logit_scale, logit_bias):
    image_norm, image_unit, image_send = unit_rows(image_embed)
    report_norm, report_unit, report_send = unit_rows(report_embed)
    scale = logit_scale[0]
    bias = logit_bias[0]
    total_bits = lax.axis_size("blk").bit_length() - 1
    image_count = (total_bits + 1) // 2
    report_list = list(range(total_bits - image_count))
    image_list = list(range(total_bits - image_count, total_bits))
    block_position = lax.axis_index("blk")
    images, image_ids = (image_send, image_study)
    for bit in image_list:
        upper = block_position >> bit & 1 == 1
        other_rows, other_ids = (
            from_partner(images, "blk", bit),
            from_partner(shortened(image_ids), "blk", bit).astype(image_ids.dtype),
        )
        images = placed(upper, images, other_rows)
        image_ids = placed(upper, image_ids, other_ids)
    reports, report_index_list = (report_send, report_study_index)
    for bit in report_list:
        upper = block_position >> bit & 1 == 1
        other_rows, other_ids = (
            from_partner(reports, "blk", bit),
            from_partner(shortened(report_index_list), "blk", bit).astype(report_index_list.dtype),
        )
        reports = placed(upper, reports, other_rows)
        report_index_list = placed(upper, report_index_list, other_ids)
    image_total = images.shape[0]
    width = images.shape[1]
    block_rows = math.gcd(image_total, 512)
    block_count = image_total // block_rows
    image_blocks = images.reshape(block_count, block_rows, width)
    id_blocks = image_ids.reshape(block_count, block_rows)

    def step(carry, input_arrays):
        report_acc, loss_acc = carry
        block_slice, study_labels = input_arrays
        logits = (
            scale
            * lax.dot_general(
                block_slice, reports, (((1,), (1,)), ((), ())), preferred_element_type=jnp.float32
            )
            + bias
        )
        pair_sign = jnp.where(
            study_labels[:, None] == report_index_list[None, :], 1.0, -1.0
        ).astype(jnp.float32)
        loss_acc = loss_acc - jnp.sum(jax.nn.log_sigmoid(pair_sign * logits))
        coeff = (-pair_sign * jax.nn.sigmoid(-pair_sign * logits)).astype(jnp.bfloat16)
        image_part = scale * jnp.dot(coeff, reports, preferred_element_type=jnp.float32)
        report_acc = report_acc + scale * lax.dot_general(
            coeff, block_slice, (((0,), (0,)), ((), ())), preferred_element_type=jnp.float32
        )
        return ((report_acc, loss_acc), image_part)

    start = (jnp.zeros((reports.shape[0], width), jnp.float32), jnp.zeros((), jnp.float32))
    (report_part, loss_part), image_parts = lax.scan(step, start, (image_blocks, id_blocks))
    image_part = image_parts.reshape(image_total, width)
    for bit in reversed(image_list):
        upper = block_position >> bit & 1 == 1
        half = image_part.shape[0] // 2
        keep = jnp.where(upper, image_part[half:], image_part[:half])
        give = jnp.where(upper, image_part[:half], image_part[half:])
        image_part = keep + from_partner(give, "blk", bit)
    for bit in reversed(report_list):
        upper = block_position >> bit & 1 == 1
        half = report_part.shape[0] // 2
        keep = jnp.where(upper, report_part[half:], report_part[:half])
        give = jnp.where(upper, report_part[:half], report_part[half:])
        report_part = keep + from_partner(give, "blk", bit)
    total = lax.psum(loss_part, "blk")
    pair_count = image_embed.shape[0] * lax.axis_size("blk")
    loss = (total / pair_count).reshape(1)
    image_grad = finish(image_part, image_unit, image_norm)
    report_grad = finish(report_part, report_unit, report_norm)
    return (loss, image_grad, report_grad)


CORE, ACROSS, NEAR, FAR = (1, 2, 4, 8)
PIECES = 4
TOP = 32767.0
MESH_ID = pl.DeviceIdType.MESH


def turned(column, rows):
    square = jnp.broadcast_to(column, (column.shape[0], rows))
    return jnp.concatenate([square] * (rows // column.shape[0]), axis=0).T


def encode(value, code_ref, step_ref):
    peak = jnp.maximum(jnp.max(jnp.abs(value), axis=1, keepdims=True), 1e-30)
    code_ref[...] = jnp.round(value * (TOP / peak)).astype(jnp.int32).astype(jnp.int16)
    step_ref[...] = turned(peak * (1.0 / TOP), step_ref.shape[1])[:8]


def decode(code_ref, step_ref):
    code = code_ref[...].astype(jnp.int32).astype(jnp.float32)
    rows = step_ref.shape[1]
    step = jnp.broadcast_to(step_ref[0:1, :], (rows, rows)).T[: code.shape[0], :1]
    return code * step


def tile_kernel(
    image_hbm, report_hbm, image_id_hbm, report_id_hbm, scale_ref, bias_ref,
    loss_ref, image_grad_ref, report_grad_ref,
    image_ref, report_ref, image_id_ref, report_id_ref,
    images, reports, image_ids, report_ids, coeffs, image_part, report_part, core_in,
    codes_out, codes_in, steps_out, steps_in, loss_out, loss_in,
    load_sem, send_sem, recv_sem,
):
    group = lax.axis_index("groups")
    me = lax.axis_index("blk")
    rows = image_ref.shape[0]
    piece = rows // PIECES

    def partner(bit):
        low = lax.rem(lax.div(me, bit), 2)
        return (group, me + bit - 2 * bit * low)

    def send(number, source, target, bit):
        copy = pltpu.make_async_remote_copy(
            src_ref=source,
            dst_ref=target,
            send_sem=send_sem.at[number],
            recv_sem=recv_sem.at[number],
            device_id=partner(bit),
            device_id_type=MESH_ID,
        )
        copy.start()
        return copy

    loads = []
    for source, target in (
        (report_hbm, report_ref),
        (image_hbm, image_ref),
        (report_id_hbm, report_id_ref),
        (image_id_hbm, image_id_ref),
    ):
        loads.append(pltpu.make_async_copy(source, target, load_sem.at[len(loads)]))
        loads[-1].start()
    barrier = pltpu.get_barrier_semaphore()
    for bit in (CORE, ACROSS, NEAR, FAR):
        pl.semaphore_signal(barrier, inc=1, device_id=partner(bit), device_id_type=MESH_ID)

    def normalised(ref):
        values = ref[...].astype(jnp.float32)
        norm = jnp.sqrt(jnp.sum(values * values, axis=1, keepdims=True) + 1e-06)
        return (norm, values / norm)

    loads[0].wait()
    reports[0] = normalised(report_ref)[1].astype(jnp.bfloat16)
    loads[1].wait()
    images[0] = normalised(image_ref)[1].astype(jnp.bfloat16)
    loads[2].wait()
    loads[3].wait()
    image_ids[0] = jnp.broadcast_to(image_id_ref[...], (8, rows))
    report_ids[0] = jnp.broadcast_to(report_id_ref[...], (8, rows))
    pl.semaphore_wait(barrier, 4)

    def part(k):
        return pl.ds(k * piece, piece)

    def near_piece(k):
        return send(32 + k, reports.at[0, part(k)], reports.at[2, part(k)], NEAR)

    report_near = [near_piece(0), near_piece(1)]
    report_near_id = send(1, report_ids.at[0], report_ids.at[2], NEAR)
    report_across = send(2, reports.at[0], reports.at[1], ACROSS)
    report_across_id = send(3, report_ids.at[0], report_ids.at[1], ACROSS)
    image_far = send(4, images.at[0], images.at[2], FAR)
    image_far_id = send(5, image_ids.at[0], image_ids.at[2], FAR)
    image_core = send(6, images.at[0], images.at[1], CORE)
    image_core_id = send(7, image_ids.at[0], image_ids.at[1], CORE)

    scale = scale_ref[0]
    bias = bias_ref[0]

    def tile(i, j):
        logits = (
            scale
            * lax.dot_general(
                images[i], reports[j], (((1,), (1,)), ((), ())), preferred_element_type=jnp.float32
            )
            + bias
        )
        across = jnp.broadcast_to(report_ids[j, 0:1, :], (rows, rows))
        down = jnp.broadcast_to(image_ids[i, 0:1, :], (rows, rows)).T
        sign = jnp.where(across == down, 1.0, -1.0).astype(jnp.float32)
        signed = sign * logits
        weight = jnp.exp(-jnp.abs(signed))
        negative = jnp.where(signed >= 0, weight, 1.0) / (1.0 + weight)
        coeffs[i, :, j * rows : (j + 1) * rows] = (-sign * negative).astype(jnp.bfloat16)
        return jnp.maximum(-signed, 0.0) + jnp.log1p(weight)

    image_core.wait()
    image_core_id.wait()
    total = tile(0, 0) + tile(1, 0)
    report_near_id.wait()
    report_diag_id = send(9, report_ids.at[2], report_ids.at[3], ACROSS)
    report_diag = []
    for k in range(PIECES):
        report_near[k].wait()
        if k + 2 < PIECES:
            report_near.append(near_piece(k + 2))
        report_diag.append(
            send(32 + PIECES + k, reports.at[2, part(k)], reports.at[3, part(k)], ACROSS)
        )
    total += tile(0, 2) + tile(1, 2)
    report_across.wait()
    report_across_id.wait()
    total += tile(0, 1) + tile(1, 1)
    image_far.wait()
    image_far_id.wait()
    image_diag = send(10, images.at[2], images.at[3], CORE)
    image_diag_id = send(11, image_ids.at[2], image_ids.at[3], CORE)
    total += tile(2, 0) + tile(2, 1) + tile(2, 2)
    image_diag.wait()
    image_diag_id.wait()
    total += tile(3, 0) + tile(3, 1) + tile(3, 2)
    def report_sum(j):
        out = None
        for i in range(4):
            term = lax.dot_general(
                coeffs[i, :, j * rows : (j + 1) * rows],
                images[i],
                (((0,), (0,)), ((), ())),
                preferred_element_type=jnp.float32,
            )
            out = term if out is None else out + term
        return scale * out

    def coded(number, height, bit):
        slot, first = divmod(number, PIECES)
        lines = pl.ds(first * height, height)
        return [
            send(40 + 2 * number, steps_out.at[number], steps_in.at[number], bit),
            send(
                41 + 2 * number, codes_out.at[slot, lines], codes_in.at[slot, lines], bit
            ),
        ]

    def put(number, value):
        slot, first = divmod(number, PIECES)
        height = value.shape[0]
        encode(value, codes_out.at[slot, pl.ds(first * height, height)], steps_out.at[number])

    def receive(copies, number, height):
        slot, first = divmod(number, PIECES)
        for copy in copies:
            copy.wait()
        return decode(codes_in.at[slot, pl.ds(first * height, height)], steps_in.at[number])

    def loss_step(step):
        return send(
            22 + step, loss_out.at[step], loss_in.at[step], (CORE, ACROSS, NEAR, FAR)[step]
        )

    across_sum = report_sum(1)
    for k in range(PIECES):
        put(2 * PIECES + k, across_sum[k * piece : (k + 1) * piece])
    report_part[1] = report_sum(2)
    early = reports[:3].reshape(3 * rows, images.shape[2])
    for i in (3, 2, 1, 0):
        image_part[i] = scale * jnp.dot(
            coeffs[i, :, : 3 * rows], early, preferred_element_type=jnp.float32
        )

    def image_sum(i):
        return image_part[i] + scale * jnp.dot(
            coeffs[i, :, 3 * rows :], reports[3], preferred_element_type=jnp.float32
        )

    for copy in report_diag:
        copy.wait()
    report_diag_id.wait()
    across_second = [coded(2 * PIECES + k, piece, ACROSS) for k in range(2)]
    for i in range(4):
        total += tile(i, 3)
    loss_out[0] = jnp.sum(total.reshape(rows // 8, 8, rows), axis=0)
    loss_copy = loss_step(0)
    reports_sum = report_sum(3)
    for k in range(PIECES):
        put(k, reports_sum[k * piece : (k + 1) * piece])
    across_first = [coded(k, piece, ACROSS) for k in range(2)]
    image_part[3] = image_sum(3)
    core_first = send(20, image_part.at[3], core_in.at[0], CORE)
    image_part[2] = image_sum(2)
    loss_copy.wait()
    loss_out[1] = loss_out[0] + loss_in[0]
    loss_copy = loss_step(1)
    core_first.wait()
    put(3 * PIECES, image_part[2] + core_in[0])
    far = coded(3 * PIECES, rows, FAR)
    near = []
    for k in range(PIECES):
        landed = receive(across_first[k], k, piece)
        put(PIECES + k, report_part[1, part(k)] + landed)
        near.append(coded(PIECES + k, piece, NEAR))
        if k + 2 < PIECES:
            across_first.append(coded(k + 2, piece, ACROSS))
        else:
            across_second.append(coded(2 * PIECES + k, piece, ACROSS))
        if k == 0:
            image_part[1] = image_sum(1)
            core_second = send(21, image_part.at[1], core_in.at[1], CORE)
        elif k == 1:
            loss_copy.wait()
            loss_out[2] = loss_out[1] + loss_in[1]
            loss_copy = loss_step(2)
        elif k == 2:
            own_image = image_sum(0)
        else:
            own_report = report_sum(0)
    loss_copy.wait()
    loss_out[3] = loss_out[2] + loss_in[2]
    loss_copy = loss_step(3)

    def finish(ref, unit_grad):
        norm, unit = normalised(ref)
        return (unit_grad - unit * jnp.sum(unit * unit_grad, axis=1, keepdims=True)) / norm

    core_second.wait()
    own_image += core_in[1]
    image_grad_ref[...] = finish(image_ref, own_image + receive(far, 3 * PIECES, rows))
    loss_copy.wait()
    pairs = rows * lax.axis_size("blk")
    loss = jnp.sum(loss_out[3] + loss_in[3]) / pairs
    loss_ref[...] = jnp.full(loss_ref.shape, loss, jnp.float32)
    report_part[0] = own_report
    for k in range(PIECES):
        report_part[0, part(k)] += receive(across_second[k], 2 * PIECES + k, piece)
    for k in range(PIECES):
        report_part[0, part(k)] += receive(near[k], PIECES + k, piece)
    report_grad_ref[...] = finish(report_ref, report_part[0])


def kernel_body(image_embed, report_embed, image_study, report_study_index, logit_scale, logit_bias):
    rows, width = image_embed.shape
    f32 = jnp.float32

    vmem = pl.BlockSpec(memory_space=pltpu.VMEM)
    hbm = pl.BlockSpec(memory_space=pltpu.HBM)
    smem = pl.BlockSpec(memory_space=pltpu.SMEM)
    loss, image_grad, report_grad = pl.pallas_call(
        tile_kernel,
        out_shape=(
            jax.ShapeDtypeStruct((8, 128), f32),
            jax.ShapeDtypeStruct((rows, width), f32),
            jax.ShapeDtypeStruct((rows, width), f32),
        ),
        in_specs=[hbm, hbm, hbm, hbm, smem, smem],
        out_specs=(vmem, vmem, vmem),
        scratch_shapes=[
            pltpu.VMEM((rows, width), jnp.bfloat16),
            pltpu.VMEM((rows, width), jnp.bfloat16),
            pltpu.VMEM((1, rows), jnp.int32),
            pltpu.VMEM((1, rows), jnp.int32),
            pltpu.VMEM((4, rows, width), jnp.bfloat16),
            pltpu.VMEM((4, rows, width), jnp.bfloat16),
            pltpu.VMEM((4, 8, rows), jnp.int32),
            pltpu.VMEM((4, 8, rows), jnp.int32),
            pltpu.VMEM((4, rows, 4 * rows), jnp.bfloat16),
            pltpu.VMEM((4, rows, width), f32),
            pltpu.VMEM((2, rows, width), f32),
            pltpu.VMEM((2, rows, width), f32),
            pltpu.VMEM((4, rows, width), jnp.int16),
            pltpu.VMEM((4, rows, width), jnp.int16),
            pltpu.VMEM((4 * PIECES, 8, rows), f32),
            pltpu.VMEM((4 * PIECES, 8, rows), f32),
            pltpu.VMEM((4, 8, rows), f32),
            pltpu.VMEM((4, 8, rows), f32),
            pltpu.SemaphoreType.DMA((4,)),
            pltpu.SemaphoreType.DMA((40 + 8 * PIECES,)),
            pltpu.SemaphoreType.DMA((40 + 8 * PIECES,)),
        ],
        compiler_params=pltpu.CompilerParams(
            collective_id=0, has_side_effects=True, vmem_limit_bytes=48 * 1024 * 1024
        ),
    )(
        pltpu.with_memory_space_constraint(image_embed, pltpu.HBM),
        pltpu.with_memory_space_constraint(report_embed, pltpu.HBM),
        pltpu.with_memory_space_constraint(image_study.reshape(1, rows), pltpu.HBM),
        pltpu.with_memory_space_constraint(report_study_index.reshape(1, rows), pltpu.HBM),
        logit_scale,
        logit_bias,
    )
    return (loss[0, :1], image_grad, report_grad)


def solution(mesh):
    return jax.shard_map(
        kernel_body if mesh.shape["blk"] == 16 else body,
        mesh=mesh,
        in_specs=(
            P(("groups", "blk"), None),
            P(("groups", "blk"), None),
            P(("groups", "blk")),
            P(("groups", "blk")),
            P("groups"),
            P("groups"),
        ),
        out_specs=(P("groups"), P(("groups", "blk"), None), P(("groups", "blk"), None)),
        check_vma=False,
    )
```

```python
import math

import jax
import jax.numpy as jnp
from jax import lax
from jax.experimental import pallas as pl
from jax.experimental.pallas import tpu as pltpu
from jax.sharding import PartitionSpec as P


def shortened(value):

    def short(part):
        return part.astype(jnp.bfloat16) if part.dtype == jnp.float32 else part

    return jax.tree.map(short, value)


def from_partner(value, axis, stride):
    return lax.ppermute(value, axis, [(i, i ^ 1 << stride) for i in range(lax.axis_size(axis))])


def unit_rows(embed):
    values = embed.astype(jnp.float32)
    norm = jnp.sqrt(jnp.sum(values * values, axis=1, keepdims=True) + 1e-06)
    unit = values / norm
    return (norm, unit, unit.astype(jnp.bfloat16))


def finish(unit_grad, unit, norm):
    return (unit_grad - unit * jnp.sum(unit * unit_grad, axis=1, keepdims=True)) / norm


def placed(upper, mine, theirs):
    return jnp.where(
        upper, jnp.concatenate([theirs, mine], axis=0), jnp.concatenate([mine, theirs], axis=0)
    )


def body(image_embed, report_embed, image_study, report_study_index, logit_scale, logit_bias):
    image_norm, image_unit, image_send = unit_rows(image_embed)
    report_norm, report_unit, report_send = unit_rows(report_embed)
    scale = logit_scale[0]
    bias = logit_bias[0]
    total_bits = lax.axis_size("blk").bit_length() - 1
    image_count = (total_bits + 1) // 2
    report_list = list(range(total_bits - image_count))
    image_list = list(range(total_bits - image_count, total_bits))
    block_position = lax.axis_index("blk")
    images, image_ids = (image_send, image_study)
    for bit in image_list:
        upper = block_position >> bit & 1 == 1
        other_rows, other_ids = (
            from_partner(images, "blk", bit),
            from_partner(shortened(image_ids), "blk", bit).astype(image_ids.dtype),
        )
        images = placed(upper, images, other_rows)
        image_ids = placed(upper, image_ids, other_ids)
    reports, report_index_list = (report_send, report_study_index)
    for bit in report_list:
        upper = block_position >> bit & 1 == 1
        other_rows, other_ids = (
            from_partner(reports, "blk", bit),
            from_partner(shortened(report_index_list), "blk", bit).astype(report_index_list.dtype),
        )
        reports = placed(upper, reports, other_rows)
        report_index_list = placed(upper, report_index_list, other_ids)
    image_total = images.shape[0]
    width = images.shape[1]
    block_rows = math.gcd(image_total, 512)
    block_count = image_total // block_rows
    image_blocks = images.reshape(block_count, block_rows, width)
    id_blocks = image_ids.reshape(block_count, block_rows)

    def step(carry, input_arrays):
        report_acc, loss_acc = carry
        block_slice, study_labels = input_arrays
        logits = (
            scale
            * lax.dot_general(
                block_slice, reports, (((1,), (1,)), ((), ())), preferred_element_type=jnp.float32
            )
            + bias
        )
        pair_sign = jnp.where(
            study_labels[:, None] == report_index_list[None, :], 1.0, -1.0
        ).astype(jnp.float32)
        loss_acc = loss_acc - jnp.sum(jax.nn.log_sigmoid(pair_sign * logits))
        coeff = (-pair_sign * jax.nn.sigmoid(-pair_sign * logits)).astype(jnp.bfloat16)
        image_part = scale * jnp.dot(coeff, reports, preferred_element_type=jnp.float32)
        report_acc = report_acc + scale * lax.dot_general(
            coeff, block_slice, (((0,), (0,)), ((), ())), preferred_element_type=jnp.float32
        )
        return ((report_acc, loss_acc), image_part)

    start = (jnp.zeros((reports.shape[0], width), jnp.float32), jnp.zeros((), jnp.float32))
    (report_part, loss_part), image_parts = lax.scan(step, start, (image_blocks, id_blocks))
    image_part = image_parts.reshape(image_total, width)
    for bit in reversed(image_list):
        upper = block_position >> bit & 1 == 1
        half = image_part.shape[0] // 2
        keep = jnp.where(upper, image_part[half:], image_part[:half])
        give = jnp.where(upper, image_part[:half], image_part[half:])
        image_part = keep + from_partner(give, "blk", bit)
    for bit in reversed(report_list):
        upper = block_position >> bit & 1 == 1
        half = report_part.shape[0] // 2
        keep = jnp.where(upper, report_part[half:], report_part[:half])
        give = jnp.where(upper, report_part[:half], report_part[half:])
        report_part = keep + from_partner(give, "blk", bit)
    total = lax.psum(loss_part, "blk")
    pair_count = image_embed.shape[0] * lax.axis_size("blk")
    loss = (total / pair_count).reshape(1)
    image_grad = finish(image_part, image_unit, image_norm)
    report_grad = finish(report_part, report_unit, report_norm)
    return (loss, image_grad, report_grad)


CORE, ACROSS, NEAR, FAR = (1, 2, 4, 8)
PIECES = 4
TOP = 32767.0
MESH_ID = pl.DeviceIdType.MESH


def turned(column, rows):
    square = jnp.broadcast_to(column, (column.shape[0], rows))
    return jnp.concatenate([square] * (rows // column.shape[0]), axis=0).T


def encode(value, code_ref, step_ref):
    peak = jnp.maximum(jnp.max(jnp.abs(value), axis=1, keepdims=True), 1e-30)
    code_ref[...] = jnp.round(value * (TOP / peak)).astype(jnp.int32).astype(jnp.int16)
    step_ref[...] = turned(peak * (1.0 / TOP), step_ref.shape[1])[:8]


def decode(code_ref, step_ref):
    code = code_ref[...].astype(jnp.int32).astype(jnp.float32)
    rows = step_ref.shape[1]
    step = jnp.broadcast_to(step_ref[0:1, :], (rows, rows)).T[: code.shape[0], :1]
    return code * step


def tile_kernel(
    image_hbm, report_hbm, image_id_hbm, report_id_hbm, scale_ref, bias_ref,
    loss_ref, image_grad_ref, report_grad_ref,
    image_ref, report_ref, image_id_ref, report_id_ref,
    images, reports, image_ids, report_ids, coeffs, image_part, report_part, core_in,
    codes_out, codes_in, steps_out, steps_in, loss_out, loss_in,
    load_sem, send_sem, recv_sem,
):
    group = lax.axis_index("groups")
    me = lax.axis_index("blk")
    rows = image_ref.shape[0]
    piece = rows // PIECES

    def partner(bit):
        low = lax.rem(lax.div(me, bit), 2)
        return (group, me + bit - 2 * bit * low)

    def send(number, source, target, bit):
        copy = pltpu.make_async_remote_copy(
            src_ref=source,
            dst_ref=target,
            send_sem=send_sem.at[number],
            recv_sem=recv_sem.at[number],
            device_id=partner(bit),
            device_id_type=MESH_ID,
        )
        copy.start()
        return copy

    loads = []
    for source, target in (
        (report_hbm, report_ref),
        (image_hbm, image_ref),
        (report_id_hbm, report_id_ref),
        (image_id_hbm, image_id_ref),
    ):
        loads.append(pltpu.make_async_copy(source, target, load_sem.at[len(loads)]))
        loads[-1].start()
    barrier = pltpu.get_barrier_semaphore()
    for bit in (CORE, ACROSS, NEAR, FAR):
        pl.semaphore_signal(barrier, inc=1, device_id=partner(bit), device_id_type=MESH_ID)

    def normalised(ref):
        values = ref[...].astype(jnp.float32)
        norm = jnp.sqrt(jnp.sum(values * values, axis=1, keepdims=True) + 1e-06)
        return (norm, values / norm)

    loads[0].wait()
    reports[0] = normalised(report_ref)[1].astype(jnp.bfloat16)
    loads[1].wait()
    images[0] = normalised(image_ref)[1].astype(jnp.bfloat16)
    loads[2].wait()
    loads[3].wait()
    image_ids[0] = jnp.broadcast_to(image_id_ref[...], (8, rows))
    report_ids[0] = jnp.broadcast_to(report_id_ref[...], (8, rows))
    pl.semaphore_wait(barrier, 4)

    def part(k):
        return pl.ds(k * piece, piece)

    def near_piece(k):
        return send(32 + k, reports.at[0, part(k)], reports.at[2, part(k)], NEAR)

    report_near = [near_piece(0), near_piece(1)]
    report_near_id = send(1, report_ids.at[0], report_ids.at[2], NEAR)
    report_across = send(2, reports.at[0], reports.at[1], ACROSS)
    report_across_id = send(3, report_ids.at[0], report_ids.at[1], ACROSS)
    image_far = send(4, images.at[0], images.at[2], FAR)
    image_far_id = send(5, image_ids.at[0], image_ids.at[2], FAR)
    image_core = send(6, images.at[0], images.at[1], CORE)
    image_core_id = send(7, image_ids.at[0], image_ids.at[1], CORE)

    scale = scale_ref[0]
    bias = bias_ref[0]

    def tile(i, j):
        logits = (
            scale
            * lax.dot_general(
                images[i], reports[j], (((1,), (1,)), ((), ())), preferred_element_type=jnp.float32
            )
            + bias
        )
        across = jnp.broadcast_to(report_ids[j, 0:1, :], (rows, rows))
        down = jnp.broadcast_to(image_ids[i, 0:1, :], (rows, rows)).T
        sign = jnp.where(across == down, 1.0, -1.0).astype(jnp.float32)
        signed = sign * logits
        weight = jnp.exp(-jnp.abs(signed))
        negative = jnp.where(signed >= 0, weight, 1.0) / (1.0 + weight)
        coeffs[i, :, j * rows : (j + 1) * rows] = (-sign * negative).astype(jnp.bfloat16)
        return jnp.maximum(-signed, 0.0) + jnp.log1p(weight)

    image_core.wait()
    image_core_id.wait()
    total = tile(0, 0) + tile(1, 0)
    report_near_id.wait()
    report_diag_id = send(9, report_ids.at[2], report_ids.at[3], ACROSS)
    report_diag = []
    for k in range(PIECES):
        report_near[k].wait()
        if k + 2 < PIECES:
            report_near.append(near_piece(k + 2))
        report_diag.append(
            send(32 + PIECES + k, reports.at[2, part(k)], reports.at[3, part(k)], ACROSS)
        )
    total += tile(0, 2) + tile(1, 2)
    report_across.wait()
    report_across_id.wait()
    total += tile(0, 1) + tile(1, 1)
    image_far.wait()
    image_far_id.wait()
    image_diag = send(10, images.at[2], images.at[3], CORE)
    image_diag_id = send(11, image_ids.at[2], image_ids.at[3], CORE)
    total += tile(2, 0) + tile(2, 1) + tile(2, 2)
    for copy in report_diag:
        copy.wait()
    report_diag_id.wait()
    total += tile(0, 3) + tile(1, 3) + tile(2, 3)
    image_diag.wait()
    image_diag_id.wait()
    total += tile(3, 3)

    def report_sum(j):
        out = None
        for i in range(4):
            term = lax.dot_general(
                coeffs[i, :, j * rows : (j + 1) * rows],
                images[i],
                (((0,), (0,)), ((), ())),
                preferred_element_type=jnp.float32,
            )
            out = term if out is None else out + term
        return scale * out

    def image_sum(i):
        return scale * jnp.dot(
            coeffs[i],
            reports[...].reshape(4 * rows, images.shape[2]),
            preferred_element_type=jnp.float32,
        )

    def coded(number, height, bit):
        slot, first = divmod(number, PIECES)
        lines = pl.ds(first * height, height)
        return [
            send(40 + 2 * number, steps_out.at[number], steps_in.at[number], bit),
            send(
                41 + 2 * number, codes_out.at[slot, lines], codes_in.at[slot, lines], bit
            ),
        ]

    def put(number, value):
        slot, first = divmod(number, PIECES)
        height = value.shape[0]
        encode(value, codes_out.at[slot, pl.ds(first * height, height)], steps_out.at[number])

    def receive(copies, number, height):
        slot, first = divmod(number, PIECES)
        for copy in copies:
            copy.wait()
        return decode(codes_in.at[slot, pl.ds(first * height, height)], steps_in.at[number])

    def loss_step(step):
        return send(
            22 + step, loss_out.at[step], loss_in.at[step], (CORE, ACROSS, NEAR, FAR)[step]
        )

    across_sum = report_sum(3)
    for k in range(PIECES):
        put(k, across_sum[k * piece : (k + 1) * piece])
    across_first = [coded(k, piece, ACROSS) for k in range(3)]
    total += tile(3, 0) + tile(3, 1) + tile(3, 2)
    image_part[0] = image_sum(3)
    core_first = send(20, image_part.at[0], core_in.at[0], CORE)
    loss_out[0] = jnp.sum(total.reshape(rows // 8, 8, rows), axis=0)
    loss_copy = loss_step(0)
    image_part[2] = image_sum(2)
    core_first.wait()
    put(3 * PIECES, image_part[2] + core_in[0])
    far = coded(3 * PIECES, rows, FAR)
    report_part[1] = report_sum(2)
    across_second = []
    near = []
    for k in range(PIECES):
        landed = receive(across_first[k], k, piece)
        if k == 0:
            across_first.append(coded(3, piece, ACROSS))
        put(PIECES + k, report_part[1, part(k)] + landed)
        near.append(coded(PIECES + k, piece, NEAR))
        if k == 0:
            across_sum = report_sum(1)
            for n in range(PIECES):
                put(2 * PIECES + n, across_sum[n * piece : (n + 1) * piece])
        else:
            across_second.append(coded(2 * PIECES + k - 1, piece, ACROSS))
    across_second.append(coded(3 * PIECES - 1, piece, ACROSS))
    image_part[1] = image_sum(1)
    core_second = send(21, image_part.at[1], core_in.at[1], CORE)
    loss_copy.wait()
    loss_out[1] = loss_out[0] + loss_in[0]
    loss_copy = loss_step(1)
    own_image = image_sum(0)
    loss_copy.wait()
    loss_out[2] = loss_out[1] + loss_in[1]
    loss_copy = loss_step(2)
    report_part[0] = report_sum(0)
    core_second.wait()
    own_image += core_in[1]
    loss_copy.wait()
    loss_out[3] = loss_out[2] + loss_in[2]
    loss_copy = loss_step(3)
    for k in range(2):
        report_part[0, part(k)] += receive(across_second[k], 2 * PIECES + k, piece)
        report_part[0, part(k)] += receive(near[k], PIECES + k, piece)

    def finish(ref, unit_grad):
        norm, unit = normalised(ref)
        return (unit_grad - unit * jnp.sum(unit * unit_grad, axis=1, keepdims=True)) / norm

    image_grad_ref[...] = finish(image_ref, own_image + receive(far, 3 * PIECES, rows))
    loss_copy.wait()
    pairs = rows * lax.axis_size("blk")
    loss = jnp.sum(loss_out[3] + loss_in[3]) / pairs
    loss_ref[...] = jnp.full(loss_ref.shape, loss, jnp.float32)
    for k in range(2, PIECES):
        report_part[0, part(k)] += receive(near[k], PIECES + k, piece)
        report_part[0, part(k)] += receive(across_second[k], 2 * PIECES + k, piece)
    report_grad_ref[...] = finish(report_ref, report_part[0])


def kernel_body(image_embed, report_embed, image_study, report_study_index, logit_scale, logit_bias):
    rows, width = image_embed.shape
    f32 = jnp.float32

    vmem = pl.BlockSpec(memory_space=pltpu.VMEM)
    hbm = pl.BlockSpec(memory_space=pltpu.HBM)
    smem = pl.BlockSpec(memory_space=pltpu.SMEM)
    loss, image_grad, report_grad = pl.pallas_call(
        tile_kernel,
        out_shape=(
            jax.ShapeDtypeStruct((8, 128), f32),
            jax.ShapeDtypeStruct((rows, width), f32),
            jax.ShapeDtypeStruct((rows, width), f32),
        ),
        in_specs=[hbm, hbm, hbm, hbm, smem, smem],
        out_specs=(vmem, vmem, vmem),
        scratch_shapes=[
            pltpu.VMEM((rows, width), jnp.bfloat16),
            pltpu.VMEM((rows, width), jnp.bfloat16),
            pltpu.VMEM((1, rows), jnp.int32),
            pltpu.VMEM((1, rows), jnp.int32),
            pltpu.VMEM((4, rows, width), jnp.bfloat16),
            pltpu.VMEM((4, rows, width), jnp.bfloat16),
            pltpu.VMEM((4, 8, rows), jnp.int32),
            pltpu.VMEM((4, 8, rows), jnp.int32),
            pltpu.VMEM((4, rows, 4 * rows), jnp.bfloat16),
            pltpu.VMEM((3, rows, width), f32),
            pltpu.VMEM((2, rows, width), f32),
            pltpu.VMEM((2, rows, width), f32),
            pltpu.VMEM((4, rows, width), jnp.int16),
            pltpu.VMEM((4, rows, width), jnp.int16),
            pltpu.VMEM((4 * PIECES, 8, rows), f32),
            pltpu.VMEM((4 * PIECES, 8, rows), f32),
            pltpu.VMEM((4, 8, rows), f32),
            pltpu.VMEM((4, 8, rows), f32),
            pltpu.SemaphoreType.DMA((4,)),
            pltpu.SemaphoreType.DMA((40 + 8 * PIECES,)),
            pltpu.SemaphoreType.DMA((40 + 8 * PIECES,)),
        ],
        compiler_params=pltpu.CompilerParams(
            collective_id=0, has_side_effects=True, vmem_limit_bytes=48 * 1024 * 1024
        ),
    )(
        pltpu.with_memory_space_constraint(image_embed, pltpu.HBM),
        pltpu.with_memory_space_constraint(report_embed, pltpu.HBM),
        pltpu.with_memory_space_constraint(image_study.reshape(1, rows), pltpu.HBM),
        pltpu.with_memory_space_constraint(report_study_index.reshape(1, rows), pltpu.HBM),
        logit_scale,
        logit_bias,
    )
    return (loss[0, :1], image_grad, report_grad)


def solution(mesh):
    return jax.shard_map(
        kernel_body if mesh.shape["blk"] == 16 else body,
        mesh=mesh,
        in_specs=(
            P(("groups", "blk"), None),
            P(("groups", "blk"), None),
            P(("groups", "blk")),
            P(("groups", "blk")),
            P("groups"),
            P("groups"),
        ),
        out_specs=(P("groups"), P(("groups", "blk"), None), P(("groups", "blk"), None)),
        check_vma=False,
    )
```

```python
import math

import jax
import jax.numpy as jnp
from jax import lax
from jax.experimental import pallas as pl
from jax.experimental.pallas import tpu as pltpu
from jax.sharding import PartitionSpec as P


def shortened(value):

    def short(part):
        return part.astype(jnp.bfloat16) if part.dtype == jnp.float32 else part

    return jax.tree.map(short, value)


def from_partner(value, axis, stride):
    return lax.ppermute(value, axis, [(i, i ^ 1 << stride) for i in range(lax.axis_size(axis))])


def unit_rows(embed):
    values = embed.astype(jnp.float32)
    norm = jnp.sqrt(jnp.sum(values * values, axis=1, keepdims=True) + 1e-06)
    unit = values / norm
    return (norm, unit, unit.astype(jnp.bfloat16))


def finish(unit_grad, unit, norm):
    return (unit_grad - unit * jnp.sum(unit * unit_grad, axis=1, keepdims=True)) / norm


def placed(upper, mine, theirs):
    return jnp.where(
        upper, jnp.concatenate([theirs, mine], axis=0), jnp.concatenate([mine, theirs], axis=0)
    )


def body(image_embed, report_embed, image_study, report_study_index, logit_scale, logit_bias):
    image_norm, image_unit, image_send = unit_rows(image_embed)
    report_norm, report_unit, report_send = unit_rows(report_embed)
    scale = logit_scale[0]
    bias = logit_bias[0]
    total_bits = lax.axis_size("blk").bit_length() - 1
    image_count = (total_bits + 1) // 2
    report_list = list(range(total_bits - image_count))
    image_list = list(range(total_bits - image_count, total_bits))
    block_position = lax.axis_index("blk")
    images, image_ids = (image_send, image_study)
    for bit in image_list:
        upper = block_position >> bit & 1 == 1
        other_rows, other_ids = (
            from_partner(images, "blk", bit),
            from_partner(shortened(image_ids), "blk", bit).astype(image_ids.dtype),
        )
        images = placed(upper, images, other_rows)
        image_ids = placed(upper, image_ids, other_ids)
    reports, report_index_list = (report_send, report_study_index)
    for bit in report_list:
        upper = block_position >> bit & 1 == 1
        other_rows, other_ids = (
            from_partner(reports, "blk", bit),
            from_partner(shortened(report_index_list), "blk", bit).astype(report_index_list.dtype),
        )
        reports = placed(upper, reports, other_rows)
        report_index_list = placed(upper, report_index_list, other_ids)
    image_total = images.shape[0]
    width = images.shape[1]
    block_rows = math.gcd(image_total, 512)
    block_count = image_total // block_rows
    image_blocks = images.reshape(block_count, block_rows, width)
    id_blocks = image_ids.reshape(block_count, block_rows)

    def step(carry, input_arrays):
        report_acc, loss_acc = carry
        block_slice, study_labels = input_arrays
        logits = (
            scale
            * lax.dot_general(
                block_slice, reports, (((1,), (1,)), ((), ())), preferred_element_type=jnp.float32
            )
            + bias
        )
        pair_sign = jnp.where(
            study_labels[:, None] == report_index_list[None, :], 1.0, -1.0
        ).astype(jnp.float32)
        loss_acc = loss_acc - jnp.sum(jax.nn.log_sigmoid(pair_sign * logits))
        coeff = (-pair_sign * jax.nn.sigmoid(-pair_sign * logits)).astype(jnp.bfloat16)
        image_part = scale * jnp.dot(coeff, reports, preferred_element_type=jnp.float32)
        report_acc = report_acc + scale * lax.dot_general(
            coeff, block_slice, (((0,), (0,)), ((), ())), preferred_element_type=jnp.float32
        )
        return ((report_acc, loss_acc), image_part)

    start = (jnp.zeros((reports.shape[0], width), jnp.float32), jnp.zeros((), jnp.float32))
    (report_part, loss_part), image_parts = lax.scan(step, start, (image_blocks, id_blocks))
    image_part = image_parts.reshape(image_total, width)
    for bit in reversed(image_list):
        upper = block_position >> bit & 1 == 1
        half = image_part.shape[0] // 2
        keep = jnp.where(upper, image_part[half:], image_part[:half])
        give = jnp.where(upper, image_part[:half], image_part[half:])
        image_part = keep + from_partner(give, "blk", bit)
    for bit in reversed(report_list):
        upper = block_position >> bit & 1 == 1
        half = report_part.shape[0] // 2
        keep = jnp.where(upper, report_part[half:], report_part[:half])
        give = jnp.where(upper, report_part[:half], report_part[half:])
        report_part = keep + from_partner(give, "blk", bit)
    total = lax.psum(loss_part, "blk")
    pair_count = image_embed.shape[0] * lax.axis_size("blk")
    loss = (total / pair_count).reshape(1)
    image_grad = finish(image_part, image_unit, image_norm)
    report_grad = finish(report_part, report_unit, report_norm)
    return (loss, image_grad, report_grad)


CORE, ACROSS, NEAR, FAR = (1, 2, 4, 8)
PIECES = 4
TOP = 32767.0
MESH_ID = pl.DeviceIdType.MESH


def turned(column, rows):
    square = jnp.broadcast_to(column, (column.shape[0], rows))
    return jnp.concatenate([square] * (rows // column.shape[0]), axis=0).T


def encode(value, code_ref, step_ref):
    peak = jnp.maximum(jnp.max(jnp.abs(value), axis=1, keepdims=True), 1e-30)
    code_ref[...] = jnp.round(value * (TOP / peak)).astype(jnp.int32).astype(jnp.int16)
    step_ref[...] = turned(peak * (1.0 / TOP), step_ref.shape[1])[:8]


def decode(code_ref, step_ref):
    code = code_ref[...].astype(jnp.int32).astype(jnp.float32)
    rows = step_ref.shape[1]
    step = jnp.broadcast_to(step_ref[0:1, :], (rows, rows)).T[: code.shape[0], :1]
    return code * step


def tile_kernel(
    image_hbm, report_hbm, image_id_hbm, report_id_hbm, scale_ref, bias_ref,
    loss_ref, image_grad_ref, report_grad_ref,
    image_ref, report_ref, image_id_ref, report_id_ref,
    images, reports, image_ids, report_ids, coeffs, image_part, report_part, core_in,
    codes_out, codes_in, steps_out, steps_in, loss_out, loss_in,
    load_sem, send_sem, recv_sem,
):
    group = lax.axis_index("groups")
    me = lax.axis_index("blk")
    rows = image_ref.shape[0]
    piece = rows // PIECES

    def partner(bit):
        low = lax.rem(lax.div(me, bit), 2)
        return (group, me + bit - 2 * bit * low)

    def send(number, source, target, bit):
        copy = pltpu.make_async_remote_copy(
            src_ref=source,
            dst_ref=target,
            send_sem=send_sem.at[number],
            recv_sem=recv_sem.at[number],
            device_id=partner(bit),
            device_id_type=MESH_ID,
        )
        copy.start()
        return copy

    loads = []
    for source, target in (
        (report_hbm, report_ref),
        (image_hbm, image_ref),
        (report_id_hbm, report_id_ref),
        (image_id_hbm, image_id_ref),
    ):
        loads.append(pltpu.make_async_copy(source, target, load_sem.at[len(loads)]))
        loads[-1].start()
    barrier = pltpu.get_barrier_semaphore()
    for bit in (CORE, ACROSS, NEAR, FAR):
        pl.semaphore_signal(barrier, inc=1, device_id=partner(bit), device_id_type=MESH_ID)

    def normalised(ref):
        values = ref[...].astype(jnp.float32)
        norm = jnp.sqrt(jnp.sum(values * values, axis=1, keepdims=True) + 1e-06)
        return (norm, values / norm)

    loads[0].wait()
    reports[0] = normalised(report_ref)[1].astype(jnp.bfloat16)
    loads[1].wait()
    images[0] = normalised(image_ref)[1].astype(jnp.bfloat16)
    loads[2].wait()
    loads[3].wait()
    image_ids[0] = jnp.broadcast_to(image_id_ref[...], (8, rows))
    report_ids[0] = jnp.broadcast_to(report_id_ref[...], (8, rows))
    pl.semaphore_wait(barrier, 4)

    def part(k):
        return pl.ds(k * piece, piece)

    def near_piece(k):
        return send(32 + k, reports.at[0, part(k)], reports.at[2, part(k)], NEAR)

    report_near = [near_piece(0), near_piece(1)]
    report_near_id = send(1, report_ids.at[0], report_ids.at[2], NEAR)
    report_across = send(2, reports.at[0], reports.at[1], ACROSS)
    report_across_id = send(3, report_ids.at[0], report_ids.at[1], ACROSS)
    image_far = send(4, images.at[0], images.at[2], FAR)
    image_far_id = send(5, image_ids.at[0], image_ids.at[2], FAR)
    image_core = send(6, images.at[0], images.at[1], CORE)
    image_core_id = send(7, image_ids.at[0], image_ids.at[1], CORE)

    scale = scale_ref[0]
    bias = bias_ref[0]

    def tile(i, j):
        logits = (
            scale
            * lax.dot_general(
                images[i], reports[j], (((1,), (1,)), ((), ())), preferred_element_type=jnp.float32
            )
            + bias
        )
        across = jnp.broadcast_to(report_ids[j, 0:1, :], (rows, rows))
        down = jnp.broadcast_to(image_ids[i, 0:1, :], (rows, rows)).T
        sign = jnp.where(across == down, 1.0, -1.0).astype(jnp.float32)
        signed = sign * logits
        weight = jnp.exp(-jnp.abs(signed))
        negative = jnp.where(signed >= 0, weight, 1.0) / (1.0 + weight)
        coeffs[i, :, j * rows : (j + 1) * rows] = (-sign * negative).astype(jnp.bfloat16)
        return jnp.maximum(-signed, 0.0) + jnp.log1p(weight)

    image_core.wait()
    image_core_id.wait()
    total = tile(0, 0) + tile(1, 0)
    report_near_id.wait()
    report_diag_id = send(9, report_ids.at[2], report_ids.at[3], ACROSS)
    report_diag = []
    for k in range(PIECES):
        report_near[k].wait()
        if k + 2 < PIECES:
            report_near.append(near_piece(k + 2))
        report_diag.append(
            send(32 + PIECES + k, reports.at[2, part(k)], reports.at[3, part(k)], ACROSS)
        )
    total += tile(0, 2) + tile(1, 2)
    report_across.wait()
    report_across_id.wait()
    total += tile(0, 1) + tile(1, 1)
    image_far.wait()
    image_far_id.wait()
    image_diag = send(10, images.at[2], images.at[3], CORE)
    image_diag_id = send(11, image_ids.at[2], image_ids.at[3], CORE)
    total += tile(2, 0) + tile(2, 1) + tile(2, 2)
    for copy in report_diag:
        copy.wait()
    report_diag_id.wait()
    total += tile(0, 3) + tile(1, 3) + tile(2, 3)
    def report_terms(j, blocks):
        out = None
        for i in blocks:
            term = lax.dot_general(
                coeffs[i, :, j * rows : (j + 1) * rows],
                images[i],
                (((0,), (0,)), ((), ())),
                preferred_element_type=jnp.float32,
            )
            out = term if out is None else out + term
        return scale * out

    def report_sum(j):
        return report_terms(j, range(4))

    def image_sum(i):
        return scale * jnp.dot(
            coeffs[i],
            reports[...].reshape(4 * rows, images.shape[2]),
            preferred_element_type=jnp.float32,
        )

    image_part[2] = image_sum(2)
    report_part[0] = report_terms(3, range(3))
    image_diag.wait()
    image_diag_id.wait()
    total += tile(3, 3)

    def coded(number, height, bit):
        slot, first = divmod(number, PIECES)
        lines = pl.ds(first * height, height)
        return [
            send(40 + 2 * number, steps_out.at[number], steps_in.at[number], bit),
            send(
                41 + 2 * number, codes_out.at[slot, lines], codes_in.at[slot, lines], bit
            ),
        ]

    def put(number, value):
        slot, first = divmod(number, PIECES)
        height = value.shape[0]
        encode(value, codes_out.at[slot, pl.ds(first * height, height)], steps_out.at[number])

    def receive(copies, number, height):
        slot, first = divmod(number, PIECES)
        for copy in copies:
            copy.wait()
        return decode(codes_in.at[slot, pl.ds(first * height, height)], steps_in.at[number])

    def loss_step(step):
        return send(
            22 + step, loss_out.at[step], loss_in.at[step], (CORE, ACROSS, NEAR, FAR)[step]
        )

    across_sum = report_part[0] + report_terms(3, (3,))
    for k in range(PIECES):
        put(k, across_sum[k * piece : (k + 1) * piece])
    across_first = [coded(k, piece, ACROSS) for k in range(3)]
    total += tile(3, 0) + tile(3, 1) + tile(3, 2)
    image_part[0] = image_sum(3)
    core_first = send(20, image_part.at[0], core_in.at[0], CORE)
    loss_out[0] = jnp.sum(total.reshape(rows // 8, 8, rows), axis=0)
    loss_copy = loss_step(0)
    report_part[1] = report_sum(2)
    core_first.wait()
    put(3 * PIECES, image_part[2] + core_in[0])
    far = coded(3 * PIECES, rows, FAR)
    across_second = []
    near = []
    for k in range(PIECES):
        landed = receive(across_first[k], k, piece)
        if k == 0:
            across_first.append(coded(3, piece, ACROSS))
        put(PIECES + k, report_part[1, part(k)] + landed)
        near.append(coded(PIECES + k, piece, NEAR))
        if k == 0:
            across_sum = report_sum(1)
            for n in range(PIECES):
                put(2 * PIECES + n, across_sum[n * piece : (n + 1) * piece])
        else:
            across_second.append(coded(2 * PIECES + k - 1, piece, ACROSS))
        if k == 1 or k == 3:
            step = k // 2
            loss_copy.wait()
            loss_out[step + 1] = loss_out[step] + loss_in[step]
            loss_copy = loss_step(step + 1)
        if k == 2:
            image_part[1] = image_sum(1)
            core_second = send(21, image_part.at[1], core_in.at[1], CORE)
    across_second.append(coded(3 * PIECES - 1, piece, ACROSS))
    own_image = image_sum(0)
    report_part[0] = report_sum(0)
    core_second.wait()
    own_image += core_in[1]
    loss_copy.wait()
    loss_out[3] = loss_out[2] + loss_in[2]
    loss_copy = loss_step(3)
    for k in range(2):
        report_part[0, part(k)] += receive(across_second[k], 2 * PIECES + k, piece)
        report_part[0, part(k)] += receive(near[k], PIECES + k, piece)

    def finish(ref, unit_grad):
        norm, unit = normalised(ref)
        return (unit_grad - unit * jnp.sum(unit * unit_grad, axis=1, keepdims=True)) / norm

    image_grad_ref[...] = finish(image_ref, own_image + receive(far, 3 * PIECES, rows))
    for k in range(2, PIECES):
        report_part[0, part(k)] += receive(near[k], PIECES + k, piece)
        report_part[0, part(k)] += receive(across_second[k], 2 * PIECES + k, piece)
    report_grad_ref[...] = finish(report_ref, report_part[0])
    loss_copy.wait()
    pairs = rows * lax.axis_size("blk")
    loss = jnp.sum(loss_out[3] + loss_in[3]) / pairs
    loss_ref[...] = jnp.full(loss_ref.shape, loss, jnp.float32)


def kernel_body(image_embed, report_embed, image_study, report_study_index, logit_scale, logit_bias):
    rows, width = image_embed.shape
    f32 = jnp.float32

    vmem = pl.BlockSpec(memory_space=pltpu.VMEM)
    hbm = pl.BlockSpec(memory_space=pltpu.HBM)
    smem = pl.BlockSpec(memory_space=pltpu.SMEM)
    loss, image_grad, report_grad = pl.pallas_call(
        tile_kernel,
        out_shape=(
            jax.ShapeDtypeStruct((8, 128), f32),
            jax.ShapeDtypeStruct((rows, width), f32),
            jax.ShapeDtypeStruct((rows, width), f32),
        ),
        in_specs=[hbm, hbm, hbm, hbm, smem, smem],
        out_specs=(vmem, vmem, vmem),
        scratch_shapes=[
            pltpu.VMEM((rows, width), jnp.bfloat16),
            pltpu.VMEM((rows, width), jnp.bfloat16),
            pltpu.VMEM((1, rows), jnp.int32),
            pltpu.VMEM((1, rows), jnp.int32),
            pltpu.VMEM((4, rows, width), jnp.bfloat16),
            pltpu.VMEM((4, rows, width), jnp.bfloat16),
            pltpu.VMEM((4, 8, rows), jnp.int32),
            pltpu.VMEM((4, 8, rows), jnp.int32),
            pltpu.VMEM((4, rows, 4 * rows), jnp.bfloat16),
            pltpu.VMEM((3, rows, width), f32),
            pltpu.VMEM((2, rows, width), f32),
            pltpu.VMEM((2, rows, width), f32),
            pltpu.VMEM((4, rows, width), jnp.int16),
            pltpu.VMEM((4, rows, width), jnp.int16),
            pltpu.VMEM((4 * PIECES, 8, rows), f32),
            pltpu.VMEM((4 * PIECES, 8, rows), f32),
            pltpu.VMEM((4, 8, rows), f32),
            pltpu.VMEM((4, 8, rows), f32),
            pltpu.SemaphoreType.DMA((4,)),
            pltpu.SemaphoreType.DMA((40 + 8 * PIECES,)),
            pltpu.SemaphoreType.DMA((40 + 8 * PIECES,)),
        ],
        compiler_params=pltpu.CompilerParams(
            collective_id=0, has_side_effects=True, vmem_limit_bytes=48 * 1024 * 1024
        ),
    )(
        pltpu.with_memory_space_constraint(image_embed, pltpu.HBM),
        pltpu.with_memory_space_constraint(report_embed, pltpu.HBM),
        pltpu.with_memory_space_constraint(image_study.reshape(1, rows), pltpu.HBM),
        pltpu.with_memory_space_constraint(report_study_index.reshape(1, rows), pltpu.HBM),
        logit_scale,
        logit_bias,
    )
    return (loss[0, :1], image_grad, report_grad)


def solution(mesh):
    return jax.shard_map(
        kernel_body if mesh.shape["blk"] == 16 else body,
        mesh=mesh,
        in_specs=(
            P(("groups", "blk"), None),
            P(("groups", "blk"), None),
            P(("groups", "blk")),
            P(("groups", "blk")),
            P("groups"),
            P("groups"),
        ),
        out_specs=(P("groups"), P(("groups", "blk"), None), P(("groups", "blk"), None)),
        check_vma=False,
    )
```

```python
import math

import jax
import jax.numpy as jnp
from jax import lax
from jax.experimental import pallas as pl
from jax.experimental.pallas import tpu as pltpu
from jax.sharding import PartitionSpec as P


def shortened(value):

    def short(part):
        return part.astype(jnp.bfloat16) if part.dtype == jnp.float32 else part

    return jax.tree.map(short, value)


def from_partner(value, axis, stride):
    return lax.ppermute(value, axis, [(i, i ^ 1 << stride) for i in range(lax.axis_size(axis))])


def unit_rows(embed):
    values = embed.astype(jnp.float32)
    norm = jnp.sqrt(jnp.sum(values * values, axis=1, keepdims=True) + 1e-06)
    unit = values / norm
    return (norm, unit, unit.astype(jnp.bfloat16))


def finish(unit_grad, unit, norm):
    return (unit_grad - unit * jnp.sum(unit * unit_grad, axis=1, keepdims=True)) / norm


def placed(upper, mine, theirs):
    return jnp.where(
        upper, jnp.concatenate([theirs, mine], axis=0), jnp.concatenate([mine, theirs], axis=0)
    )


def body(image_embed, report_embed, image_study, report_study_index, logit_scale, logit_bias):
    image_norm, image_unit, image_send = unit_rows(image_embed)
    report_norm, report_unit, report_send = unit_rows(report_embed)
    scale = logit_scale[0]
    bias = logit_bias[0]
    total_bits = lax.axis_size("blk").bit_length() - 1
    image_count = (total_bits + 1) // 2
    report_list = list(range(total_bits - image_count))
    image_list = list(range(total_bits - image_count, total_bits))
    block_position = lax.axis_index("blk")
    images, image_ids = (image_send, image_study)
    for bit in image_list:
        upper = block_position >> bit & 1 == 1
        other_rows, other_ids = (
            from_partner(images, "blk", bit),
            from_partner(shortened(image_ids), "blk", bit).astype(image_ids.dtype),
        )
        images = placed(upper, images, other_rows)
        image_ids = placed(upper, image_ids, other_ids)
    reports, report_index_list = (report_send, report_study_index)
    for bit in report_list:
        upper = block_position >> bit & 1 == 1
        other_rows, other_ids = (
            from_partner(reports, "blk", bit),
            from_partner(shortened(report_index_list), "blk", bit).astype(report_index_list.dtype),
        )
        reports = placed(upper, reports, other_rows)
        report_index_list = placed(upper, report_index_list, other_ids)
    image_total = images.shape[0]
    width = images.shape[1]
    block_rows = math.gcd(image_total, 512)
    block_count = image_total // block_rows
    image_blocks = images.reshape(block_count, block_rows, width)
    id_blocks = image_ids.reshape(block_count, block_rows)

    def step(carry, input_arrays):
        report_acc, loss_acc = carry
        block_slice, study_labels = input_arrays
        logits = (
            scale
            * lax.dot_general(
                block_slice, reports, (((1,), (1,)), ((), ())), preferred_element_type=jnp.float32
            )
            + bias
        )
        pair_sign = jnp.where(
            study_labels[:, None] == report_index_list[None, :], 1.0, -1.0
        ).astype(jnp.float32)
        loss_acc = loss_acc - jnp.sum(jax.nn.log_sigmoid(pair_sign * logits))
        coeff = (-pair_sign * jax.nn.sigmoid(-pair_sign * logits)).astype(jnp.bfloat16)
        image_part = scale * jnp.dot(coeff, reports, preferred_element_type=jnp.float32)
        report_acc = report_acc + scale * lax.dot_general(
            coeff, block_slice, (((0,), (0,)), ((), ())), preferred_element_type=jnp.float32
        )
        return ((report_acc, loss_acc), image_part)

    start = (jnp.zeros((reports.shape[0], width), jnp.float32), jnp.zeros((), jnp.float32))
    (report_part, loss_part), image_parts = lax.scan(step, start, (image_blocks, id_blocks))
    image_part = image_parts.reshape(image_total, width)
    for bit in reversed(image_list):
        upper = block_position >> bit & 1 == 1
        half = image_part.shape[0] // 2
        keep = jnp.where(upper, image_part[half:], image_part[:half])
        give = jnp.where(upper, image_part[:half], image_part[half:])
        image_part = keep + from_partner(give, "blk", bit)
    for bit in reversed(report_list):
        upper = block_position >> bit & 1 == 1
        half = report_part.shape[0] // 2
        keep = jnp.where(upper, report_part[half:], report_part[:half])
        give = jnp.where(upper, report_part[:half], report_part[half:])
        report_part = keep + from_partner(give, "blk", bit)
    total = lax.psum(loss_part, "blk")
    pair_count = image_embed.shape[0] * lax.axis_size("blk")
    loss = (total / pair_count).reshape(1)
    image_grad = finish(image_part, image_unit, image_norm)
    report_grad = finish(report_part, report_unit, report_norm)
    return (loss, image_grad, report_grad)


CORE, ACROSS, NEAR, FAR = (1, 2, 4, 8)
PIECES = 4
TOP = 32767.0
MESH_ID = pl.DeviceIdType.MESH


def turned(column, rows):
    square = jnp.broadcast_to(column, (column.shape[0], rows))
    return jnp.concatenate([square] * (rows // column.shape[0]), axis=0).T


def encode(value, code_ref, step_ref):
    peak = jnp.maximum(jnp.max(jnp.abs(value), axis=1, keepdims=True), 1e-30)
    code_ref[...] = jnp.round(value * (TOP / peak)).astype(jnp.int32).astype(jnp.int16)
    step_ref[...] = turned(peak * (1.0 / TOP), step_ref.shape[1])[:8]


def decode(code_ref, step_ref):
    code = code_ref[...].astype(jnp.int32).astype(jnp.float32)
    rows = step_ref.shape[1]
    step = jnp.broadcast_to(step_ref[0:1, :], (rows, rows)).T[: code.shape[0], :1]
    return code * step


def tile_kernel(
    image_hbm, report_hbm, image_id_hbm, report_id_hbm, scale_ref, bias_ref,
    loss_ref, image_grad_ref, report_grad_ref,
    image_ref, report_ref, image_id_ref, report_id_ref,
    images, reports, image_ids, report_ids, coeffs, image_part, report_part, core_in,
    codes_out, codes_in, steps_out, steps_in, loss_out, loss_in,
    load_sem, send_sem, recv_sem,
):
    group = lax.axis_index("groups")
    me = lax.axis_index("blk")
    rows = image_ref.shape[0]
    started = []
    piece = rows // PIECES

    def partner(bit):
        low = lax.rem(lax.div(me, bit), 2)
        return (group, me + bit - 2 * bit * low)

    def send(number, source, target, bit):
        copy = pltpu.make_async_remote_copy(
            src_ref=source,
            dst_ref=target,
            send_sem=send_sem.at[number],
            recv_sem=recv_sem.at[number],
            device_id=partner(bit),
            device_id_type=MESH_ID,
        )
        copy.start()
        started.append(copy)
        return copy

    loads = []
    for source, target in (
        (report_hbm, report_ref),
        (image_hbm, image_ref),
        (report_id_hbm, report_id_ref),
        (image_id_hbm, image_id_ref),
    ):
        loads.append(pltpu.make_async_copy(source, target, load_sem.at[len(loads)]))
        loads[-1].start()
    barrier = pltpu.get_barrier_semaphore()
    for bit in (CORE, ACROSS, NEAR, FAR):
        pl.semaphore_signal(barrier, inc=1, device_id=partner(bit), device_id_type=MESH_ID)

    def normalised(ref):
        values = ref[...].astype(jnp.float32)
        norm = jnp.sqrt(jnp.sum(values * values, axis=1, keepdims=True) + 1e-06)
        return (norm, values / norm)

    loads[0].wait()
    reports[0] = normalised(report_ref)[1].astype(jnp.bfloat16)
    loads[1].wait()
    images[0] = normalised(image_ref)[1].astype(jnp.bfloat16)
    loads[2].wait()
    loads[3].wait()
    image_ids[0] = jnp.broadcast_to(image_id_ref[...], (8, rows))
    report_ids[0] = jnp.broadcast_to(report_id_ref[...], (8, rows))
    pl.semaphore_wait(barrier, 4)

    def part(k):
        return pl.ds(k * piece, piece)

    def near_piece(k):
        return send(32 + k, reports.at[0, part(k)], reports.at[2, part(k)], NEAR)

    def across_piece(k):
        return send(24 + 2 + k, reports.at[0, part(k)], reports.at[1, part(k)], ACROSS)

    def far_piece(k):
        return send(40 + 8 * PIECES + k, images.at[0, part(k)], images.at[2, part(k)], FAR)

    report_near, report_across, image_far = ([], [], [])
    report_near_id = send(1, report_ids.at[0], report_ids.at[2], NEAR)
    report_across_id = send(3, report_ids.at[0], report_ids.at[1], ACROSS)
    image_far_id = send(5, image_ids.at[0], image_ids.at[2], FAR)
    for k in range(PIECES):
        report_near.append(near_piece(k))
        image_far.append(far_piece(k))
        report_across.append(across_piece(k))
    image_core = send(6, images.at[0], images.at[1], CORE)
    image_core_id = send(7, image_ids.at[0], image_ids.at[1], CORE)

    scale = scale_ref[0]
    bias = bias_ref[0]

    def tile(i, j):
        logits = (
            scale
            * lax.dot_general(
                images[i], reports[j], (((1,), (1,)), ((), ())), preferred_element_type=jnp.float32
            )
            + bias
        )
        across = jnp.broadcast_to(report_ids[j, 0:1, :], (rows, rows))
        down = jnp.broadcast_to(image_ids[i, 0:1, :], (rows, rows)).T
        sign = jnp.where(across == down, 1.0, -1.0).astype(jnp.float32)
        signed = sign * logits
        weight = jnp.exp(-jnp.abs(signed))
        negative = jnp.where(signed >= 0, weight, 1.0) / (1.0 + weight)
        coeffs[i, :, j * rows : (j + 1) * rows] = (-sign * negative).astype(jnp.bfloat16)
        return jnp.maximum(-signed, 0.0) + jnp.log1p(weight)

    image_core.wait_recv()
    image_core_id.wait_recv()
    total = tile(0, 0) + tile(1, 0)
    report_near_id.wait_recv()
    report_diag_id = send(9, report_ids.at[2], report_ids.at[3], ACROSS)
    report_diag = []
    for k in range(PIECES):
        report_near[k].wait_recv()
        report_diag.append(
            send(32 + PIECES + k, reports.at[2, part(k)], reports.at[3, part(k)], ACROSS)
        )
    total += tile(0, 2) + tile(1, 2)
    for copy in report_across:
        copy.wait_recv()
    report_across_id.wait_recv()
    total += tile(0, 1) + tile(1, 1)
    for copy in image_far:
        copy.wait_recv()
    image_far_id.wait_recv()
    image_diag = send(10, images.at[2], images.at[3], CORE)
    image_diag_id = send(11, image_ids.at[2], image_ids.at[3], CORE)
    total += tile(2, 0) + tile(2, 1) + tile(2, 2)
    for copy in report_diag:
        copy.wait_recv()
    report_diag_id.wait_recv()
    total += tile(0, 3) + tile(1, 3) + tile(2, 3)
    def report_terms(j, blocks):
        out = None
        for i in blocks:
            term = lax.dot_general(
                coeffs[i, :, j * rows : (j + 1) * rows],
                images[i],
                (((0,), (0,)), ((), ())),
                preferred_element_type=jnp.float32,
            )
            out = term if out is None else out + term
        return scale * out

    def report_sum(j):
        return report_terms(j, range(4))

    def image_sum(i):
        return scale * jnp.dot(
            coeffs[i],
            reports[...].reshape(4 * rows, images.shape[2]),
            preferred_element_type=jnp.float32,
        )

    image_part[2] = image_sum(2)
    report_part[0] = report_terms(3, range(3))
    image_diag.wait_recv()
    image_diag_id.wait_recv()
    total += tile(3, 3)

    def coded(number, height, bit):
        slot, first = divmod(number, PIECES)
        lines = pl.ds(first * height, height)
        return [
            send(40 + 2 * number, steps_out.at[number], steps_in.at[number], bit),
            send(
                41 + 2 * number, codes_out.at[slot, lines], codes_in.at[slot, lines], bit
            ),
        ]

    def put(number, value):
        slot, first = divmod(number, PIECES)
        height = value.shape[0]
        encode(value, codes_out.at[slot, pl.ds(first * height, height)], steps_out.at[number])

    def receive(copies, number, height):
        slot, first = divmod(number, PIECES)
        for copy in copies:
            copy.wait_recv()
        return decode(codes_in.at[slot, pl.ds(first * height, height)], steps_in.at[number])

    def loss_step(step):
        return send(
            22 + step, loss_out.at[step], loss_in.at[step], (CORE, ACROSS, NEAR, FAR)[step]
        )

    across_sum = report_part[0] + report_terms(3, (3,))
    for k in range(PIECES):
        put(k, across_sum[k * piece : (k + 1) * piece])
    across_first = [coded(k, piece, ACROSS) for k in range(3)]
    total += tile(3, 0) + tile(3, 1) + tile(3, 2)
    image_part[0] = image_sum(3)
    core_first = send(20, image_part.at[0], core_in.at[0], CORE)
    loss_out[0] = jnp.sum(total.reshape(rows // 8, 8, rows), axis=0)
    loss_copy = loss_step(0)
    report_part[1] = report_sum(2)
    core_first.wait_recv()
    put(3 * PIECES, image_part[2] + core_in[0])
    far = coded(3 * PIECES, rows, FAR)
    across_second = []
    near = []
    for k in range(PIECES):
        landed = receive(across_first[k], k, piece)
        if k == 0:
            across_first.append(coded(3, piece, ACROSS))
        put(PIECES + k, report_part[1, part(k)] + landed)
        near.append(coded(PIECES + k, piece, NEAR))
        if k == 0:
            across_sum = report_sum(1)
            for n in range(PIECES):
                put(2 * PIECES + n, across_sum[n * piece : (n + 1) * piece])
        else:
            across_second.append(coded(2 * PIECES + k - 1, piece, ACROSS))
        if k == 1 or k == 3:
            step = k // 2
            loss_copy.wait_recv()
            loss_out[step + 1] = loss_out[step] + loss_in[step]
            loss_copy = loss_step(step + 1)
        if k == 2:
            image_part[1] = image_sum(1)
            core_second = send(21, image_part.at[1], core_in.at[1], CORE)
    across_second.append(coded(3 * PIECES - 1, piece, ACROSS))
    own_image = image_sum(0)
    report_part[0] = report_sum(0)
    core_second.wait_recv()
    own_image += core_in[1]
    loss_copy.wait_recv()
    loss_out[3] = loss_out[2] + loss_in[2]
    loss_copy = loss_step(3)
    for k in range(2):
        report_part[0, part(k)] += receive(across_second[k], 2 * PIECES + k, piece)
        report_part[0, part(k)] += receive(near[k], PIECES + k, piece)

    def finish(ref, unit_grad):
        norm, unit = normalised(ref)
        return (unit_grad - unit * jnp.sum(unit * unit_grad, axis=1, keepdims=True)) / norm

    image_grad_ref[...] = finish(image_ref, own_image + receive(far, 3 * PIECES, rows))
    for k in range(2, PIECES):
        report_part[0, part(k)] += receive(near[k], PIECES + k, piece)
        report_part[0, part(k)] += receive(across_second[k], 2 * PIECES + k, piece)
    report_grad_ref[...] = finish(report_ref, report_part[0])
    loss_copy.wait_recv()
    pairs = rows * lax.axis_size("blk")
    loss = jnp.sum(loss_out[3] + loss_in[3]) / pairs
    loss_ref[...] = jnp.full(loss_ref.shape, loss, jnp.float32)
    for copy in started:
        copy.wait_send()


def kernel_body(image_embed, report_embed, image_study, report_study_index, logit_scale, logit_bias):
    rows, width = image_embed.shape
    f32 = jnp.float32

    vmem = pl.BlockSpec(memory_space=pltpu.VMEM)
    hbm = pl.BlockSpec(memory_space=pltpu.HBM)
    smem = pl.BlockSpec(memory_space=pltpu.SMEM)
    loss, image_grad, report_grad = pl.pallas_call(
        tile_kernel,
        out_shape=(
            jax.ShapeDtypeStruct((8, 128), f32),
            jax.ShapeDtypeStruct((rows, width), f32),
            jax.ShapeDtypeStruct((rows, width), f32),
        ),
        in_specs=[hbm, hbm, hbm, hbm, smem, smem],
        out_specs=(vmem, vmem, vmem),
        scratch_shapes=[
            pltpu.VMEM((rows, width), jnp.bfloat16),
            pltpu.VMEM((rows, width), jnp.bfloat16),
            pltpu.VMEM((1, rows), jnp.int32),
            pltpu.VMEM((1, rows), jnp.int32),
            pltpu.VMEM((4, rows, width), jnp.bfloat16),
            pltpu.VMEM((4, rows, width), jnp.bfloat16),
            pltpu.VMEM((4, 8, rows), jnp.int32),
            pltpu.VMEM((4, 8, rows), jnp.int32),
            pltpu.VMEM((4, rows, 4 * rows), jnp.bfloat16),
            pltpu.VMEM((3, rows, width), f32),
            pltpu.VMEM((2, rows, width), f32),
            pltpu.VMEM((2, rows, width), f32),
            pltpu.VMEM((4, rows, width), jnp.int16),
            pltpu.VMEM((4, rows, width), jnp.int16),
            pltpu.VMEM((4 * PIECES, 8, rows), f32),
            pltpu.VMEM((4 * PIECES, 8, rows), f32),
            pltpu.VMEM((4, 8, rows), f32),
            pltpu.VMEM((4, 8, rows), f32),
            pltpu.SemaphoreType.DMA((4,)),
            pltpu.SemaphoreType.DMA((40 + 9 * PIECES,)),
            pltpu.SemaphoreType.DMA((40 + 9 * PIECES,)),
        ],
        compiler_params=pltpu.CompilerParams(
            collective_id=0, has_side_effects=True, vmem_limit_bytes=48 * 1024 * 1024
        ),
    )(
        pltpu.with_memory_space_constraint(image_embed, pltpu.HBM),
        pltpu.with_memory_space_constraint(report_embed, pltpu.HBM),
        pltpu.with_memory_space_constraint(image_study.reshape(1, rows), pltpu.HBM),
        pltpu.with_memory_space_constraint(report_study_index.reshape(1, rows), pltpu.HBM),
        logit_scale,
        logit_bias,
    )
    return (loss[0, :1], image_grad, report_grad)


def solution(mesh):
    return jax.shard_map(
        kernel_body if mesh.shape["blk"] == 16 else body,
        mesh=mesh,
        in_specs=(
            P(("groups", "blk"), None),
            P(("groups", "blk"), None),
            P(("groups", "blk")),
            P(("groups", "blk")),
            P("groups"),
            P("groups"),
        ),
        out_specs=(P("groups"), P(("groups", "blk"), None), P(("groups", "blk"), None)),
        check_vma=False,
    )
```
